32 devices in a mesh: groups: 2 (over x), blocks: 4 (over y, core), heads: 4 (over z).
Axes of the slice: x: 2, y: 2, z: 4, core: 2. Of those that a mesh axis runs over, the one named last changes fastest.
Arguments:
- queries: bfloat16 [4, 64, 6144], P(None, ('groups', 'blocks'), 'heads'), parts along dimension 1, may hold values from -200 to 200
- key_cache: bfloat16 [64, 128, 6144], P(('groups', 'blocks'), None, 'heads'), parts along dimension 0, may hold values from -6 to 6
- value_cache: bfloat16 [64, 128, 6144], P(('groups', 'blocks'), None, 'heads'), parts along dimension 0, may hold values from -6 to 6
- key_new: bfloat16 [4, 64, 6144], P(None, ('groups', 'blocks'), 'heads'), parts along dimension 1, may hold values from -6 to 6
- value_new: bfloat16 [4, 64, 6144], P(None, ('groups', 'blocks'), 'heads'), parts along dimension 1, may hold values from -6 to 6
- lengths: int32 [64], P(('groups', 'blocks')), parts along dimension 0, may hold values from 32 to 128, as said below
- out_proj: bfloat16 [6144, 6144], P('heads', 'blocks'), may hold values from -0.078125 to 0.078125
- residual: bfloat16 [4, 64, 6144], P(None, 'groups', 'blocks'), parts along dimension 1, may hold values from -12 to 12
- norm_gain: bfloat16 [6144], P('blocks'), may hold values from 0.099609375 to 1.8984375
- hot_up: bfloat16 [64, 6144, 128], P('heads', 'blocks'), may hold values from -0.078125 to 0.078125
- hot_down: bfloat16 [64, 128, 6144], P('heads', None, 'blocks'), may hold values from -0.0625 to 0.0625
- cold_up: bfloat16 [32, 6144, 128], P(('blocks', 'heads')), may hold values from -0.078125 to 0.078125
- cold_down: bfloat16 [32, 128, 6144], P(('blocks', 'heads')), may hold values from -0.25 to 0.25
- block_rows: int32 [8, 4, 2, 32], P('groups', 'heads'), parts along dimension 0, may hold values from 0 to 127, as said below
- block_counts: int32 [8, 4, 2], P('groups', 'heads'), parts along dimension 0, may hold values from 1 to 32, as said below
Outputs:
- attn_state: bfloat16 [4, 64, 6144], P(None, 'groups', 'blocks'), parts along dimension 1
- ffn_out: bfloat16 [4, 64, 6144], P(None, ('groups', 'heads'), 'blocks'), parts along dimension 1
The draws below stay inside these ranges and needn't reach their ends.
There are 2 independent parts, one for each index of `groups`. The reference program is written for one: setup_inputs(seed, part) draws one part's arguments, and reference() takes and returns one part's arrays. A program takes and returns all parts, laid end to end along the dimension named above; an argument that names none is the same for every part. Nothing has to cross between parts.
Inputs may be any that keep to these rules, and one draw needn't show every extreme that they name: `block_rows`: entries beyond block_counts are 0; live entries of one list are distinct row-steps t * 32 + r. `block_counts`: some cold block has exactly 32 live entries. `lengths`: some row has all 128 slots live.
All inputs are finite; a program needn't handle non-finite values.
Results may differ from the reference program's by a relative error of at most 0.017.
Values may be sent and summed in bfloat16 or wider, within the bound.
No kernel may reach another device: no remote copies, remote signals or barrier semaphores. Data moves between devices by JAX's collectives and lax.ppermute only.
A program may use at most 128 MiB of HBM per device.

```python
import math
import jax
import jax.numpy as jnp
from jax import lax

HEADS = 48
HD = 128
HB = 128
STEPS = 4
CTX = 128
COLD_DEV = 2
HOT = 64
D = 6144
ROWS = 32
CAP = 32
NCOLD = 32
N_BLOCKS = 4
N_HEADS = 4


def shared_keys(key):
    return jnp.clip(jax.random.normal(jax.random.fold_in(key, 101), (ROWS, CTX, D), jnp.float32), -6.0, 6.0)


def draw_key_cache(key, part):
    drawn_keys = shared_keys(key)
    return drawn_keys.astype(jnp.bfloat16)


def draw_queries(key, part):
    key = jax.random.fold_in(key, 2)
    entries = jnp.clip(jax.random.normal(key, (STEPS, ROWS, D), jnp.float32), -6.0, 6.0)
    return entries.astype(jnp.bfloat16)


def draw_residual(key, part):
    key = jax.random.fold_in(key, 3)
    trend = 3.0 ** (jnp.arange(D, dtype=jnp.float32) / D)
    spread = jnp.exp(math.log(4.0) * jax.random.uniform(jax.random.fold_in(key, 1), (D,), jnp.float32))
    column_scale = 0.25 * trend * spread
    values = jnp.clip(jax.random.normal(jax.random.fold_in(key, 2), (STEPS, ROWS, D), jnp.float32), -4.0, 4.0)
    return (values * column_scale).astype(jnp.bfloat16)


def draw_lengths(key, part):
    key = jax.random.fold_in(key, 4)
    drawn = jax.random.randint(jax.random.fold_in(key, 1), (ROWS,), CTX // 4, CTX + 1)
    filled = jax.random.randint(jax.random.fold_in(key, 2), (), 0, ROWS)
    return jnp.where(jnp.arange(ROWS) == filled, CTX, drawn).astype(jnp.int32)


def routing(key):
    row_steps = STEPS * ROWS
    subkeys = jax.random.split(jax.random.fold_in(key, 201), NCOLD)

    def one_order(subkey):
        return jax.random.permutation(subkey, row_steps)[:CAP]
    orders = jax.vmap(one_order)(subkeys)
    counts = jax.random.randint(jax.random.fold_in(key, 202), (NCOLD,), 1, CAP + 1)
    filled = jax.random.randint(jax.random.fold_in(key, 203), (), 0, NCOLD)
    counts = jnp.where(jnp.arange(NCOLD) == filled, CAP, counts)
    in_use = jnp.arange(CAP)[None, :] < counts[:, None]
    orders = jnp.where(in_use, orders, 0)
    return (orders.reshape(N_BLOCKS, N_HEADS, COLD_DEV, CAP).astype(jnp.int32), counts.reshape(N_BLOCKS, N_HEADS, COLD_DEV).astype(jnp.int32))


def draw_block_rows(key, part):
    orders, counts = routing(key)
    return orders


def draw_block_counts(key, part):
    orders, counts = routing(key)
    return counts


def levels(stream_key, dims, shards, low, largest):
    def one(dim, blocks):
        heights = jax.random.uniform(jax.random.fold_in(jax.random.fold_in(stream_key, 6), dim), (blocks,), jnp.float32, low / len(shards), largest / len(shards))
        return jnp.repeat(jnp.exp(heights), dims[dim] // blocks).reshape((-1,) + (1,) * (len(dims) - dim - 1))

    gain = one(*shards[0])
    for cut in shards[1:]:
        gain = gain * one(*cut)
    return gain


def noise(stream_key, extent, width, reach, cuts=(), held_as=jnp.bfloat16):
    array = width * jax.random.normal(stream_key, extent, jnp.float32)
    if cuts:
        array = array * levels(stream_key, extent, cuts, -0.22, 0.18)
    return jnp.clip(array, -reach, reach).astype(held_as)


def setup_inputs(seed: int = 0, part: int = 0) -> dict:
    key_of = jax.random.split(jax.random.key(seed), 16)
    part_keys = jax.random.split(jax.random.fold_in(key_of[15], part), 16)
    queries = draw_queries(jax.random.fold_in(jax.random.fold_in(key_of[15], part), 71), part)
    key_cache = draw_key_cache(jax.random.fold_in(jax.random.fold_in(key_of[15], part), 71), part)
    value_cache = noise(part_keys[2], (ROWS, CTX, D), 1.0, 6.0, ((0, 4), (2, 4)))
    key_new = noise(part_keys[3], (STEPS, ROWS, D), 1.0, 6.0, ((1, 4), (2, 4)))
    value_new = noise(part_keys[4], (STEPS, ROWS, D), 1.0, 6.0, ((1, 4), (2, 4)))
    lengths = draw_lengths(jax.random.fold_in(jax.random.fold_in(key_of[15], part), 71), part)
    out_proj = noise(key_of[6], (D, D), D ** -0.5, 0.078125, ((0, 4), (1, 4)))
    residual = draw_residual(jax.random.fold_in(jax.random.fold_in(key_of[15], part), 71), part)
    norm_gain = jnp.clip(1.0 + 0.18 * jax.random.normal(key_of[8], (D,), jnp.float32), 0.099609375, 1.8984375).astype(jnp.bfloat16)
    hot_up = noise(key_of[9], (HOT, D, HB), D ** -0.5, 0.078125, ((0, 4), (1, 4)))
    hot_down = noise(key_of[10], (HOT, HB, D), (HOT * HB) ** -0.5, 0.0625, ((0, 4), (2, 4)))
    cold_up = noise(key_of[11], (NCOLD, D, HB), D ** -0.5, 0.078125, ((0, 16),))
    cold_down = noise(key_of[12], (NCOLD, HB, D), (NCOLD * HB // 8) ** -0.5, 0.25, ((0, 16),))
    block_rows = draw_block_rows(jax.random.fold_in(jax.random.fold_in(key_of[15], part), 71), part)
    block_counts = draw_block_counts(jax.random.fold_in(jax.random.fold_in(key_of[15], part), 71), part)
    return dict(queries=queries, key_cache=key_cache, value_cache=value_cache, key_new=key_new, value_new=value_new, lengths=lengths, out_proj=out_proj, residual=residual, norm_gain=norm_gain, hot_up=hot_up, hot_down=hot_down, cold_up=cold_up, cold_down=cold_down, block_rows=block_rows, block_counts=block_counts)


def reference(queries, key_cache, value_cache, key_new, value_new, lengths, out_proj, residual, norm_gain, hot_up, hot_down, cold_up, cold_down, block_rows, block_counts):
    query_heads = queries.astype(jnp.float32).reshape(STEPS, ROWS, HEADS, HD)
    cached_keys = key_cache.astype(jnp.float32).reshape(ROWS, CTX, HEADS, HD)
    cached_values = value_cache.astype(jnp.float32).reshape(ROWS, CTX, HEADS, HD)
    recent_keys = key_new.astype(jnp.float32).reshape(STEPS, ROWS, HEADS, HD)
    recent_values = value_new.astype(jnp.float32).reshape(STEPS, ROWS, HEADS, HD)
    factor = 1.0 / math.sqrt(HD)
    old_scores = jnp.einsum('trhd,rphd->trhp', query_heads, cached_keys) * factor
    visible = jnp.arange(CTX)[None, :] < lengths[:, None]
    old_scores = jnp.where(visible[None, :, None, :], old_scores, -jnp.inf)
    new_scores = jnp.einsum('trhd,srhd->trhs', query_heads, recent_keys) * factor
    causal = jnp.arange(STEPS)[None, :] <= jnp.arange(STEPS)[:, None]
    new_scores = jnp.where(causal[:, None, None, :], new_scores, -jnp.inf)
    highest = jnp.maximum(lax.optimization_barrier(jnp.max(old_scores, axis=-1)), lax.optimization_barrier(jnp.max(new_scores, axis=-1)))[..., None]
    old_weights = jnp.exp(old_scores - highest)
    new_weights = jnp.exp(new_scores - highest)
    denominator = lax.optimization_barrier(jnp.sum(old_weights, axis=-1, keepdims=True)) + lax.optimization_barrier(jnp.sum(new_weights, axis=-1, keepdims=True))
    old_probs = lax.optimization_barrier((old_weights / denominator).astype(jnp.bfloat16)).astype(jnp.float32)
    new_probs = lax.optimization_barrier((new_weights / denominator).astype(jnp.bfloat16)).astype(jnp.float32)
    attended = jnp.einsum('trhp,rphd->trhd', old_probs, cached_values) + jnp.einsum('trhs,srhd->trhd', new_probs, recent_values)
    attended = attended.reshape(STEPS * ROWS, D).astype(jnp.bfloat16)
    projected = jnp.dot(attended, out_proj, preferred_element_type=jnp.float32)
    state = (residual.reshape(STEPS * ROWS, D).astype(jnp.float32) + projected).astype(jnp.bfloat16)
    state_wide = state.astype(jnp.float32)
    mean_row = lax.optimization_barrier(jnp.mean(state_wide, axis=-1, keepdims=True))
    centred = state_wide - mean_row
    variance = lax.optimization_barrier(jnp.mean(centred * centred, axis=-1, keepdims=True))
    normed = (centred * lax.rsqrt(variance + 1e-05) * norm_gain.astype(jnp.float32)).astype(jnp.bfloat16)
    hot_in = jnp.transpose(hot_up, (1, 0, 2)).reshape(D, HOT * HB)
    hot_hidden = jnp.maximum(jnp.dot(normed, hot_in, preferred_element_type=jnp.float32), 0.0).astype(jnp.bfloat16)
    hot_sum = jnp.dot(hot_hidden, hot_down.reshape(HOT * HB, D), preferred_element_type=jnp.float32)
    row_lists = block_rows.reshape(NCOLD, CAP).astype(jnp.int32)
    live_counts = block_counts.reshape(NCOLD).astype(jnp.int32)

    def one_block(running, item):
        up_weight, down_weight, picked_rows, count = item
        picked = normed[picked_rows]
        hidden = jnp.maximum(jnp.dot(picked, up_weight, preferred_element_type=jnp.float32), 0.0).astype(jnp.bfloat16)
        piece = lax.optimization_barrier(jnp.dot(hidden, down_weight, preferred_element_type=jnp.float32).astype(jnp.bfloat16)).astype(jnp.float32)
        keep = (jnp.arange(CAP) < count)[:, None]
        return (running.at[picked_rows].add(jnp.where(keep, piece, 0.0)), None)
    cold_sum, _ = lax.scan(one_block, jnp.zeros((STEPS * ROWS, D), jnp.float32), (cold_up, cold_down, row_lists, live_counts))
    ffn_out = (hot_sum + cold_sum).astype(jnp.bfloat16).reshape(STEPS, ROWS, D)
    return (state.reshape(STEPS, ROWS, D), ffn_out)
```

```python
import functools
import math

import jax
import jax.numpy as jnp
from jax import lax
from jax.experimental import pallas as pl
from jax.experimental.pallas import tpu as pltpu
from jax.sharding import PartitionSpec as P

HD = 128
D = 6144


def local(
    queries,
    key_cache,
    value_cache,
    key_new,
    value_new,
    lengths,
    out_proj,
    residual,
    norm_gain,
    hot_up,
    hot_down,
    cold_up,
    cold_down,
    block_rows,
    block_counts,
):
    steps, rows_here, width_here = queries.shape
    heads_here = width_here // HD
    context = key_cache.shape[1]
    query_heads = queries.reshape(steps, rows_here, heads_here, HD)
    cached_keys = key_cache.reshape(rows_here, context, heads_here, HD)
    cached_values = value_cache.reshape(rows_here, context, heads_here, HD)
    recent_keys = key_new.reshape(steps, rows_here, heads_here, HD)
    recent_values = value_new.reshape(steps, rows_here, heads_here, HD)
    factor = 1.0 / math.sqrt(HD)
    old_scores = (
        jnp.einsum("trhd,rphd->trhp", query_heads, cached_keys, preferred_element_type=jnp.float32)
        * factor
    )
    visible = jnp.arange(context)[None, :] < lengths[:, None]
    old_scores = jnp.where(visible[None, :, None, :], old_scores, -jnp.inf)
    new_scores = (
        jnp.einsum("trhd,srhd->trhs", query_heads, recent_keys, preferred_element_type=jnp.float32)
        * factor
    )
    causal = jnp.arange(steps)[None, :] <= jnp.arange(steps)[:, None]
    new_scores = jnp.where(causal[:, None, None, :], new_scores, -jnp.inf)
    highest = jnp.maximum(jnp.max(old_scores, axis=-1), jnp.max(new_scores, axis=-1))[..., None]
    old_weights = jnp.exp(old_scores - highest)
    new_weights = jnp.exp(new_scores - highest)
    denominator = jnp.sum(old_weights, axis=-1, keepdims=True) + jnp.sum(
        new_weights, axis=-1, keepdims=True
    )
    old_probs = (old_weights / denominator).astype(jnp.bfloat16)
    new_probs = (new_weights / denominator).astype(jnp.bfloat16)
    attended = jnp.einsum(
        "trhp,rphd->trhd", old_probs, cached_values, preferred_element_type=jnp.float32
    )
    attended = attended + jnp.einsum(
        "trhs,srhd->trhd", new_probs, recent_values, preferred_element_type=jnp.float32
    )
    attended = attended.reshape(steps, rows_here, width_here).astype(jnp.bfloat16)
    partial_out = jnp.einsum(
        "trk,kc->trc",
        lax.all_gather(attended, "blocks", axis=1, tiled=True),
        out_proj,
        preferred_element_type=jnp.float32,
    )
    summed = lax.psum(partial_out.astype(jnp.bfloat16), "heads").astype(jnp.float32)
    state = (residual.astype(jnp.float32) + summed).astype(jnp.bfloat16)
    state_wide = state.astype(jnp.float32)
    mean_row = lax.psum(jnp.sum(state_wide, axis=-1), "blocks") / D
    centred = state_wide - mean_row[..., None]
    variance = lax.psum(jnp.sum(centred * centred, axis=-1), "blocks") / D
    normed = (
        centred * lax.rsqrt(variance + 1e-05)[..., None] * norm_gain.astype(jnp.float32)
    ).astype(jnp.bfloat16)
    hot_inputs = jnp.einsum("trc,kch->trkh", normed, hot_up, preferred_element_type=jnp.float32)
    hot_total = lax.psum(hot_inputs.astype(jnp.bfloat16), "blocks").astype(jnp.float32)
    hot_hidden = jnp.maximum(hot_total, 0.0).astype(jnp.bfloat16)
    hot_sum = jnp.einsum("trkh,khc->trc", hot_hidden, hot_down, preferred_element_type=jnp.float32)
    all_rows = normed.shape[1]
    slice_width = normed.shape[2]
    flat_rows = normed.reshape(steps * all_rows, slice_width)
    slot_rows = block_rows[:, 0]
    slot_counts = block_counts[:, 0]
    outgoing = flat_rows[slot_rows]
    hidden = jnp.maximum(
        jnp.einsum(
            "ocnd,cdh->ocnh",
            lax.all_to_all(outgoing, "blocks", split_axis=0, concat_axis=3, tiled=True),
            cold_up,
            preferred_element_type=jnp.float32,
        ),
        0.0,
    ).astype(jnp.bfloat16)
    made = jnp.einsum(
        "ocnh,chd->ocnd", hidden, cold_down, preferred_element_type=jnp.float32
    ).astype(jnp.bfloat16)
    returned = lax.all_to_all(made, "blocks", split_axis=3, concat_axis=0, tiled=True)
    keep = jnp.arange(returned.shape[2])[None, None, :] < slot_counts[..., None]
    gained = jnp.where(keep[..., None], returned.astype(jnp.float32), 0.0)
    cold_sum = (
        jnp.zeros((steps * all_rows, slice_width), jnp.float32)
        .at[slot_rows.reshape(-1)]
        .add(gained.reshape(-1, slice_width))
    )
    total = cold_sum.reshape(steps, all_rows, slice_width) + hot_sum
    ffn_out = lax.psum_scatter(total.astype(jnp.bfloat16), "heads", scatter_dimension=1, tiled=True)
    return (state, ffn_out)


def params(**more):
    return pltpu.CompilerParams(vmem_limit_bytes=40 * 2**20, **more)


def attention_kernel(lengths, q_ref, k_ref, v_ref, kn_ref, vn_ref, out_ref, *, here, steps, context):
    rows = steps * here
    wide = q_ref.shape[1]
    parts = wide // HD
    q = q_ref[...]
    lane_head = lax.broadcasted_iota(jnp.int32, (rows, wide), 1) // HD
    split = jnp.concatenate(
        [jnp.where(lane_head == i, q, jnp.zeros_like(q)) for i in range(parts)], axis=0
    )
    nt = (((1,), (1,)), ((), ()))
    scores = lax.dot_general(split, k_ref[...], nt, preferred_element_type=jnp.float32)
    row = lax.broadcasted_iota(jnp.int32, (parts * rows, context), 0) % here
    slot = lax.broadcasted_iota(jnp.int32, (parts * rows, context), 1)
    limit = jnp.zeros_like(slot)
    own = scores[:, :context]
    for r in range(here):
        limit = jnp.where(row == r, lengths[r], limit)
        if r:
            own = jnp.where(row == r, scores[:, r * context : (r + 1) * context], own)
    factor = 1.0 / math.sqrt(HD)
    own = jnp.where(slot < limit, own * factor, -jnp.inf)
    fresh = lax.dot_general(split, kn_ref[...], nt, preferred_element_type=jnp.float32) * factor
    at = lax.broadcasted_iota(jnp.int32, (parts * rows, rows), 0) % rows
    to = lax.broadcasted_iota(jnp.int32, (parts * rows, rows), 1)
    seen = (at % here == to % here) & (to // here <= at // here)
    fresh = jnp.where(seen, fresh, -jnp.inf)
    top = jnp.maximum(
        jnp.max(own, axis=-1, keepdims=True), jnp.max(fresh, axis=-1, keepdims=True)
    )
    own = jnp.exp(own - top)
    fresh = jnp.exp(fresh - top)
    scale = 1.0 / (
        jnp.sum(own, axis=-1, keepdims=True) + jnp.sum(fresh, axis=-1, keepdims=True)
    )
    own = own * scale
    spread = jnp.concatenate(
        [jnp.where(row == r, own, 0.0).astype(jnp.bfloat16) for r in range(here)], axis=1
    )
    got = jnp.dot(spread, v_ref[...], preferred_element_type=jnp.float32)
    got = got + jnp.dot(
        (fresh * scale).astype(jnp.bfloat16), vn_ref[...], preferred_element_type=jnp.float32
    )
    answer = got[:rows]
    for i in range(1, parts):
        answer = jnp.where(lane_head == i, got[i * rows : (i + 1) * rows], answer)
    out_ref[...] = answer.astype(jnp.bfloat16)


def attention(queries, key_cache, value_cache, key_new, value_new, lengths):
    steps, here, width = queries.shape
    context = key_cache.shape[1]
    wide = 2 * HD
    small = pl.BlockSpec((steps * here, wide), lambda i, *_: (0, i))
    large = pl.BlockSpec((here * context, wide), lambda i, *_: (0, i))
    flat = lambda a: a.reshape(-1, width)
    return pl.pallas_call(
        functools.partial(attention_kernel, here=here, steps=steps, context=context),
        grid_spec=pltpu.PrefetchScalarGridSpec(
            num_scalar_prefetch=1,
            grid=(width // wide,),
            in_specs=[small, large, large, small, small],
            out_specs=small,
        ),
        out_shape=jax.ShapeDtypeStruct((steps * here, width), jnp.bfloat16),
        compiler_params=params(),
        name="attention",
    )(lengths, flat(queries), flat(key_cache), flat(value_cache), flat(key_new), flat(value_new))


def project_kernel(place, rows_ref, weight_ref, *outs):
    chunk = outs[0].shape[0]
    rows = jnp.concatenate(
        [
            rows_ref[pl.ds(pl.multiple_of((place[0] ^ m) * chunk, chunk), chunk), :]
            for m in range(len(outs))
        ],
        axis=0,
    )
    made = jnp.dot(rows, weight_ref[...], preferred_element_type=jnp.float32)
    for m, out in enumerate(outs):
        out[...] = made[m * chunk : (m + 1) * chunk].astype(out.dtype)


def project(place, rows, weight, parts):
    total, depth = rows.shape
    width = weight.shape[1]
    chunk = total // parts
    wide = width // 3
    return pl.pallas_call(
        project_kernel,
        grid_spec=pltpu.PrefetchScalarGridSpec(
            num_scalar_prefetch=1,
            grid=(width // wide,),
            in_specs=[
                pl.BlockSpec((total, depth), lambda i, *_: (0, 0)),
                pl.BlockSpec((depth, wide), lambda i, *_: (0, i)),
            ],
            out_specs=[pl.BlockSpec((chunk, wide), lambda i, *_: (0, i))] * parts,
        ),
        out_shape=[
            jax.ShapeDtypeStruct((chunk, width), jnp.bfloat16 if m else jnp.float32)
            for m in range(parts)
        ],
        compiler_params=params(),
        name="project",
    )(place, rows, weight)


def join_kernel(residual, mine, *refs):
    state_ref, mean_ref, spread_ref = refs[-3:]
    total = residual[...].astype(jnp.float32) + mine[...]
    for ref in refs[:-3]:
        total = total + ref[...].astype(jnp.float32)
    state = total.astype(jnp.bfloat16)
    state_ref[...] = state
    wide = state.astype(jnp.float32)
    mean = jnp.mean(wide, axis=-1, keepdims=True)
    off = wide - mean
    mean_ref[...] = jnp.broadcast_to(mean, mean_ref.shape)
    spread_ref[...] = jnp.broadcast_to(jnp.sum(off * off, axis=-1, keepdims=True), mean_ref.shape)


def join(residual, mine, others):
    chunk, width = mine.shape
    stat = jax.ShapeDtypeStruct((chunk, HD), jnp.float32)
    return pl.pallas_call(
        join_kernel,
        out_shape=[jax.ShapeDtypeStruct((chunk, width), jnp.bfloat16), stat, stat],
        compiler_params=params(),
        name="join",
    )(residual, mine, *others)


def up_kernel(place, *refs, parts, hot_steps):
    states, stats = refs[:parts], refs[parts : 2 * parts]
    gain_ref, hot_ref, near_ref, first_ref, second_ref, out_ref, normed = refs[2 * parts :]
    step = pl.program_id(0)
    y, g = place[1], place[2]

    @pl.when(step == 0)
    def _():
        gain = gain_ref[...].astype(jnp.float32)
        chunk = states[0].shape[0]
        for m in range(parts):
            mean = stats[m][0, :, :1]
            variance = stats[m][1, :, :1] / D
            off = states[m][...].astype(jnp.float32) - mean
            normed[m * chunk : (m + 1) * chunk, :] = (
                off * lax.rsqrt(variance + 1e-05) * gain
            ).astype(jnp.bfloat16)

    def put(first, second, column):
        weight = jnp.concatenate([first, second], axis=1)
        made = jnp.dot(normed[...], weight, preferred_element_type=jnp.float32)
        at = pl.multiple_of(column * 2 * HD, 2 * HD)
        out_ref[:, pl.ds(at, 2 * HD)] = made.astype(out_ref.dtype)

    @pl.when(step < hot_steps)
    def _():
        put(hot_ref[0], hot_ref[1], step)

    @pl.when(step == hot_steps)
    def _():
        put(near_ref[g], near_ref[1 - g], hot_steps + y)

    @pl.when(step == hot_steps + 1)
    def _():
        put(first_ref[...], second_ref[...], hot_steps + 1 - y)


def up(place, half, states, stats, gain, hot, near, first, second):
    parts = len(states)
    chunk, width = states[0].shape
    hot_steps = hot.shape[0] // 4
    whole = lambda a: pl.BlockSpec(a.shape, lambda i, *_: (0,) * a.ndim)
    columns = (2 * hot_steps + 4) * HD
    return pl.pallas_call(
        functools.partial(up_kernel, parts=parts, hot_steps=hot_steps),
        grid_spec=pltpu.PrefetchScalarGridSpec(
            num_scalar_prefetch=1,
            grid=(hot_steps + 2,),
            in_specs=[whole(a) for a in states]
            + [whole(a) for a in stats]
            + [
                whole(gain),
                pl.BlockSpec(
                    (2, width, HD),
                    lambda i, place: (
                        (place[3] ^ half) * hot_steps + jnp.minimum(i, hot_steps - 1),
                        0,
                        0,
                    ),
                ),
                pl.BlockSpec((2, width, HD), lambda i, place: (0, place[4], 0)),
                whole(first),
                whole(second),
            ],
            out_specs=pl.BlockSpec((parts * chunk, columns), lambda i, *_: (0, 0)),
            scratch_shapes=[pltpu.VMEM((parts * chunk, width), jnp.bfloat16)],
        ),
        out_shape=jax.ShapeDtypeStruct((parts * chunk, columns), jnp.bfloat16),
        compiler_params=params(),
        name="up_keep" if half == 0 else "up_send",
    )(place, *states, *stats, gain, hot, near, first, second)


def down_kernel(place, hidden_ref, hot_ref, near_ref, first_ref, second_ref, *refs):
    y, g = place[1], place[2]
    blocks, depth, wide = hot_ref.shape
    made = jnp.dot(
        hidden_ref[:, : blocks * depth],
        hot_ref[...].reshape(blocks * depth, wide),
        preferred_element_type=jnp.float32,
    )

    def add(made, first, second, pair):
        at = pl.multiple_of(blocks * depth + pair * 2 * depth, 2 * depth)
        return made + jnp.dot(
            hidden_ref[:, pl.ds(at, 2 * depth)],
            jnp.concatenate([first, second], axis=0),
            preferred_element_type=jnp.float32,
        )

    made = add(made, near_ref[g], near_ref[1 - g], y)
    made = add(made, first_ref[...], second_ref[...], 1 - y)
    if len(refs) == 1:
        refs[0][...] = made
        return
    made = made + refs[0][...]
    outs = refs[1:]
    chunk = outs[0].shape[0]
    for m, out in enumerate(outs):
        out[...] = made[m * chunk : (m + 1) * chunk].astype(out.dtype)


def down(place, half, hidden, hot, near, first, second, before, parts):
    rows = hidden.shape[0]
    width = hot.shape[2]
    wide = width // 3
    per = width // wide
    blocks = hot.shape[0] // 2
    column = lambda i, *_: (0, i)
    in_specs = [
        pl.BlockSpec(hidden.shape, lambda i, *_: (0, 0)),
        pl.BlockSpec((blocks, HD, wide), lambda i, place: (place[3] ^ half, 0, i)),
        pl.BlockSpec((2, HD, wide), lambda i, place: (0, 0, place[4] * per + i)),
        pl.BlockSpec((HD, wide), column),
        pl.BlockSpec((HD, wide), column),
    ]
    operands = [hidden, hot, near, first, second]
    if before is None:
        out_specs = pl.BlockSpec((rows, wide), column)
        out_shape = jax.ShapeDtypeStruct((rows, width), jnp.float32)
    else:
        in_specs.append(pl.BlockSpec((rows, wide), column))
        operands.append(before)
        out_specs = [pl.BlockSpec((rows // parts, wide), column)] * parts
        out_shape = [
            jax.ShapeDtypeStruct((rows // parts, width), jnp.bfloat16 if m else jnp.float32)
            for m in range(parts)
        ]
    return pl.pallas_call(
        down_kernel,
        grid_spec=pltpu.PrefetchScalarGridSpec(
            num_scalar_prefetch=1, grid=(per,), in_specs=in_specs, out_specs=out_specs
        ),
        out_shape=out_shape,
        compiler_params=params(),
        name="down_keep" if half == 0 else "down_got",
    )(place, *operands)


def swap(x, axis, m, size):
    return lax.ppermute(x, axis, [(i, i ^ m) for i in range(size)])


def local_fast(
    queries,
    key_cache,
    value_cache,
    key_new,
    value_new,
    lengths,
    out_proj,
    residual,
    norm_gain,
    hot_up,
    hot_down,
    cold_up,
    cold_down,
    block_rows,
    block_counts,
):
    steps, here, _ = queries.shape
    all_rows, width = residual.shape[1:]
    n_heads = all_rows // here
    g = lax.axis_index("groups")
    b = lax.axis_index("blocks")
    h = lax.axis_index("heads")
    y, core = b // 2, b % 2
    place = jnp.stack([h, y, g, core, b]).astype(jnp.int32)

    near_up = swap(cold_up, "blocks", 1, 4)
    near_down = swap(cold_down, "blocks", 1, 4)
    far_up, far_down = {}, {}
    for m in (2, 3):
        piece = lax.dynamic_slice(cold_up, (g, (b ^ m) * width, 0), (1, width, HD))[0]
        first = swap(piece, "blocks", m, 4)
        far_up[m] = (first, swap(first, "groups", 1, 2))
    for m in (2, 3):
        piece = lax.dynamic_slice(cold_down, (g, 0, (b ^ m) * width), (1, HD, width))[0]
        first = swap(piece, "blocks", m, 4)
        far_down[m] = (first, swap(first, "groups", 1, 2))

    attended = attention(queries, key_cache, value_cache, key_new, value_new, lengths)
    gathered = lax.all_gather(attended, "blocks", axis=0, tiled=True)
    pieces = project(place, gathered, out_proj, n_heads)
    others = [swap(pieces[m], "heads", m, n_heads) for m in range(1, n_heads)]
    mine = lax.dynamic_slice(residual, (0, h * here, 0), (steps, here, width))
    state, mean, spread = join(mine.reshape(steps * here, width), pieces[0], others)
    states = [state] + [swap(state, "heads", m, n_heads) for m in range(1, n_heads)]
    stat = jnp.stack([mean, spread])
    count = width
    for m in (2, 1):
        got = swap(stat, "blocks", m, 4)
        gap = stat[0] - got[0]
        stat = jnp.stack(
            [(stat[0] + got[0]) * 0.5, stat[1] + got[1] + gap * gap * (count * 0.5)]
        )
        count = count * 2
    stats = [stat] + [swap(stat, "heads", m, n_heads) for m in range(1, n_heads)]

    index = jnp.arange(n_heads * steps * here)
    chunk = (index // (steps * here)) ^ h
    row = (index // here % steps) * all_rows + chunk * here + index % here
    pair = jnp.arange(4)
    owner = (pair // 2) * 2 + core
    slot = (pair % 2) ^ g
    lists = block_rows[:, 0][owner, slot]
    counts = block_counts[:, 0][owner, slot]
    live = jnp.arange(lists.shape[1])[None, :] < counts[:, None]
    used = jnp.any((lists[None] == row[:, None, None]) & live[None], axis=-1)
    hot_width = hot_up.shape[0] // 2 * HD
    mask = jnp.concatenate(
        [
            jnp.ones((row.shape[0], hot_width), jnp.bfloat16),
            jnp.repeat(used.astype(jnp.bfloat16), HD, axis=1),
        ],
        axis=1,
    )

    gain = norm_gain[None]
    sent = up(place, 1, states, stats, gain, hot_up, near_up, *far_up[3])
    got = swap(sent, "blocks", 1, 4)
    kept = up(place, 0, states, stats, gain, hot_up, cold_up, *far_up[2])
    summed = (kept.astype(jnp.float32) + got.astype(jnp.float32)).astype(jnp.bfloat16)
    total = summed.astype(jnp.float32) + swap(summed, "blocks", 2, 4).astype(jnp.float32)
    hidden = jnp.maximum(total, 0.0).astype(jnp.bfloat16) * mask
    partner = swap(hidden, "blocks", 1, 4)
    before = down(place, 0, hidden, hot_down, cold_down, *far_down[2], None, n_heads)
    parts = down(place, 1, partner, hot_down, near_down, *far_down[3], before, n_heads)
    out = parts[0]
    for m in range(1, n_heads):
        out = out + swap(parts[m], "heads", m, n_heads).astype(jnp.float32)
    ffn_out = out.astype(jnp.bfloat16).reshape(steps, here, width)

    stacked = jnp.stack(states).reshape(n_heads, steps, 1, here, width)
    ordered = [
        lax.dynamic_index_in_dim(stacked, c ^ h, axis=0, keepdims=False) for c in range(n_heads)
    ]
    attn_state = jnp.concatenate(ordered, axis=1).reshape(steps, all_rows, width)
    return (attn_state, ffn_out)


def solution(mesh):
    placed = (
        P(None, ("groups", "blocks"), "heads"),
        P(("groups", "blocks"), None, "heads"),
        P(("groups", "blocks"), None, "heads"),
        P(None, ("groups", "blocks"), "heads"),
        P(None, ("groups", "blocks"), "heads"),
        P(("groups", "blocks")),
        P("heads", "blocks"),
        P(None, "groups", "blocks"),
        P("blocks"),
        P("heads", "blocks", None),
        P("heads", None, "blocks"),
        P(("blocks", "heads"), None, None),
        P(("blocks", "heads"), None, None),
        P("groups", "heads", None, None),
        P("groups", "heads", None),
    )
    sizes = tuple(mesh.shape[a] for a in ("groups", "blocks", "heads"))
    return jax.shard_map(
        local_fast if sizes == (2, 4, 4) else local,
        mesh=mesh,
        in_specs=placed,
        out_specs=(P(None, "groups", "blocks"), P(None, ("groups", "heads"), "blocks")),
        check_vma=False,
    )
```

```python
import functools
import math

import jax
import jax.numpy as jnp
from jax import lax
from jax.experimental import pallas as pl
from jax.experimental.pallas import tpu as pltpu
from jax.sharding import PartitionSpec as P

HD = 128
D = 6144


def local(
    queries,
    key_cache,
    value_cache,
    key_new,
    value_new,
    lengths,
    out_proj,
    residual,
    norm_gain,
    hot_up,
    hot_down,
    cold_up,
    cold_down,
    block_rows,
    block_counts,
):
    steps, rows_here, width_here = queries.shape
    heads_here = width_here // HD
    context = key_cache.shape[1]
    query_heads = queries.reshape(steps, rows_here, heads_here, HD)
    cached_keys = key_cache.reshape(rows_here, context, heads_here, HD)
    cached_values = value_cache.reshape(rows_here, context, heads_here, HD)
    recent_keys = key_new.reshape(steps, rows_here, heads_here, HD)
    recent_values = value_new.reshape(steps, rows_here, heads_here, HD)
    factor = 1.0 / math.sqrt(HD)
    old_scores = (
        jnp.einsum("trhd,rphd->trhp", query_heads, cached_keys, preferred_element_type=jnp.float32)
        * factor
    )
    visible = jnp.arange(context)[None, :] < lengths[:, None]
    old_scores = jnp.where(visible[None, :, None, :], old_scores, -jnp.inf)
    new_scores = (
        jnp.einsum("trhd,srhd->trhs", query_heads, recent_keys, preferred_element_type=jnp.float32)
        * factor
    )
    causal = jnp.arange(steps)[None, :] <= jnp.arange(steps)[:, None]
    new_scores = jnp.where(causal[:, None, None, :], new_scores, -jnp.inf)
    highest = jnp.maximum(jnp.max(old_scores, axis=-1), jnp.max(new_scores, axis=-1))[..., None]
    old_weights = jnp.exp(old_scores - highest)
    new_weights = jnp.exp(new_scores - highest)
    denominator = jnp.sum(old_weights, axis=-1, keepdims=True) + jnp.sum(
        new_weights, axis=-1, keepdims=True
    )
    old_probs = (old_weights / denominator).astype(jnp.bfloat16)
    new_probs = (new_weights / denominator).astype(jnp.bfloat16)
    attended = jnp.einsum(
        "trhp,rphd->trhd", old_probs, cached_values, preferred_element_type=jnp.float32
    )
    attended = attended + jnp.einsum(
        "trhs,srhd->trhd", new_probs, recent_values, preferred_element_type=jnp.float32
    )
    attended = attended.reshape(steps, rows_here, width_here).astype(jnp.bfloat16)
    partial_out = jnp.einsum(
        "trk,kc->trc",
        lax.all_gather(attended, "blocks", axis=1, tiled=True),
        out_proj,
        preferred_element_type=jnp.float32,
    )
    summed = lax.psum(partial_out.astype(jnp.bfloat16), "heads").astype(jnp.float32)
    state = (residual.astype(jnp.float32) + summed).astype(jnp.bfloat16)
    state_wide = state.astype(jnp.float32)
    mean_row = lax.psum(jnp.sum(state_wide, axis=-1), "blocks") / D
    centred = state_wide - mean_row[..., None]
    variance = lax.psum(jnp.sum(centred * centred, axis=-1), "blocks") / D
    normed = (
        centred * lax.rsqrt(variance + 1e-05)[..., None] * norm_gain.astype(jnp.float32)
    ).astype(jnp.bfloat16)
    hot_inputs = jnp.einsum("trc,kch->trkh", normed, hot_up, preferred_element_type=jnp.float32)
    hot_total = lax.psum(hot_inputs.astype(jnp.bfloat16), "blocks").astype(jnp.float32)
    hot_hidden = jnp.maximum(hot_total, 0.0).astype(jnp.bfloat16)
    hot_sum = jnp.einsum("trkh,khc->trc", hot_hidden, hot_down, preferred_element_type=jnp.float32)
    all_rows = normed.shape[1]
    slice_width = normed.shape[2]
    flat_rows = normed.reshape(steps * all_rows, slice_width)
    slot_rows = block_rows[:, 0]
    slot_counts = block_counts[:, 0]
    outgoing = flat_rows[slot_rows]
    hidden = jnp.maximum(
        jnp.einsum(
            "ocnd,cdh->ocnh",
            lax.all_to_all(outgoing, "blocks", split_axis=0, concat_axis=3, tiled=True),
            cold_up,
            preferred_element_type=jnp.float32,
        ),
        0.0,
    ).astype(jnp.bfloat16)
    made = jnp.einsum(
        "ocnh,chd->ocnd", hidden, cold_down, preferred_element_type=jnp.float32
    ).astype(jnp.bfloat16)
    returned = lax.all_to_all(made, "blocks", split_axis=3, concat_axis=0, tiled=True)
    keep = jnp.arange(returned.shape[2])[None, None, :] < slot_counts[..., None]
    gained = jnp.where(keep[..., None], returned.astype(jnp.float32), 0.0)
    cold_sum = (
        jnp.zeros((steps * all_rows, slice_width), jnp.float32)
        .at[slot_rows.reshape(-1)]
        .add(gained.reshape(-1, slice_width))
    )
    total = cold_sum.reshape(steps, all_rows, slice_width) + hot_sum
    ffn_out = lax.psum_scatter(total.astype(jnp.bfloat16), "heads", scatter_dimension=1, tiled=True)
    return (state, ffn_out)


BIG = 60 * 2**20
PAD = 16


def params(limit=BIG):
    return pltpu.CompilerParams(vmem_limit_bytes=limit)


def attention_kernel(
    lengths, q_ref, k_ref, v_ref, kn_ref, vn_ref, gain_ref, out_ref, *, here, steps, context
):
    rows = steps * here
    wide = q_ref.shape[1]
    parts = wide // HD
    q = q_ref[...]
    lane_head = lax.broadcasted_iota(jnp.int32, (rows, wide), 1) // HD
    split = jnp.concatenate(
        [jnp.where(lane_head == i, q, jnp.zeros_like(q)) for i in range(parts)], axis=0
    )
    nt = (((1,), (1,)), ((), ()))
    scores = lax.dot_general(split, k_ref[...], nt, preferred_element_type=jnp.float32)
    row = lax.broadcasted_iota(jnp.int32, (parts * rows, context), 0) % here
    slot = lax.broadcasted_iota(jnp.int32, (parts * rows, context), 1)
    limit = jnp.zeros_like(slot)
    own = scores[:, :context]
    for r in range(here):
        limit = jnp.where(row == r, lengths[r], limit)
        if r:
            own = jnp.where(row == r, scores[:, r * context : (r + 1) * context], own)
    factor = 1.0 / math.sqrt(HD)
    own = jnp.where(slot < limit, own * factor, -jnp.inf)
    fresh = lax.dot_general(split, kn_ref[...], nt, preferred_element_type=jnp.float32) * factor
    at = lax.broadcasted_iota(jnp.int32, (parts * rows, rows), 0) % rows
    to = lax.broadcasted_iota(jnp.int32, (parts * rows, rows), 1)
    seen = (at % here == to % here) & (to // here <= at // here)
    fresh = jnp.where(seen, fresh, -jnp.inf)
    top = jnp.maximum(
        jnp.max(own, axis=-1, keepdims=True), jnp.max(fresh, axis=-1, keepdims=True)
    )
    own = jnp.exp(own - top)
    fresh = jnp.exp(fresh - top)
    scale = 1.0 / (
        jnp.sum(own, axis=-1, keepdims=True) + jnp.sum(fresh, axis=-1, keepdims=True)
    )
    own = own * scale
    spread = jnp.concatenate(
        [jnp.where(row == r, own, 0.0).astype(jnp.bfloat16) for r in range(here)], axis=1
    )
    got = jnp.dot(spread, v_ref[...], preferred_element_type=jnp.float32)
    got = got + jnp.dot(
        (fresh * scale).astype(jnp.bfloat16), vn_ref[...], preferred_element_type=jnp.float32
    )
    answer = got[:rows]
    for i in range(1, parts):
        answer = jnp.where(lane_head == i, got[i * rows : (i + 1) * rows], answer)
    gain = jnp.broadcast_to(gain_ref[...].astype(jnp.float32), (PAD, wide))
    out_ref[...] = jnp.concatenate([answer, gain], axis=0).astype(jnp.bfloat16)


def attention(queries, key_cache, value_cache, key_new, value_new, gain, lengths):
    steps, here, width = queries.shape
    context = key_cache.shape[1]
    wide = 2 * HD
    rows = steps * here
    column = lambda i, *_: (0, i)
    small = pl.BlockSpec((rows, wide), column)
    large = pl.BlockSpec((here * context, wide), column)
    flat = lambda a: a.reshape(-1, width)
    return pl.pallas_call(
        functools.partial(attention_kernel, here=here, steps=steps, context=context),
        grid_spec=pltpu.PrefetchScalarGridSpec(
            num_scalar_prefetch=1,
            grid=(width // wide,),
            in_specs=[small, large, large, small, small, pl.BlockSpec((1, wide), column)],
            out_specs=pl.BlockSpec((rows + PAD, wide), column),
        ),
        out_shape=jax.ShapeDtypeStruct((rows + PAD, width), jnp.bfloat16),
        compiler_params=params(),
        name="attention",
    )(
        lengths,
        flat(queries),
        flat(key_cache),
        flat(value_cache),
        flat(key_new),
        flat(value_new),
        gain,
    )


def project_kernel(place, rows_ref, weight_ref, *outs):
    chunk = outs[0].shape[0]
    rows = jnp.concatenate(
        [rows_ref[place[0] ^ m, :chunk, :] for m in range(len(outs))], axis=0
    )
    made = jnp.dot(rows, weight_ref[...], preferred_element_type=jnp.float32)
    for m, out in enumerate(outs):
        out[...] = made[m * chunk : (m + 1) * chunk].astype(out.dtype)


def project(place, gathered, weight):
    parts, padded, depth = gathered.shape
    width = weight.shape[1]
    chunk = padded - PAD
    wide = width // 3
    return pl.pallas_call(
        project_kernel,
        grid_spec=pltpu.PrefetchScalarGridSpec(
            num_scalar_prefetch=1,
            grid=(width // wide,),
            in_specs=[
                pl.BlockSpec(gathered.shape, lambda i, *_: (0, 0, 0)),
                pl.BlockSpec((depth, wide), lambda i, *_: (0, i)),
            ],
            out_specs=[pl.BlockSpec((chunk, wide), lambda i, *_: (0, i))] * parts,
        ),
        out_shape=[
            jax.ShapeDtypeStruct((chunk, width), jnp.bfloat16 if m else jnp.float32)
            for m in range(parts)
        ],
        compiler_params=params(),
        name="project",
    )(place, gathered, weight)


def join_kernel(*refs):
    total = refs[0][...].astype(jnp.float32)
    for ref in refs[1:-1]:
        total = total + ref[...].astype(jnp.float32)
    refs[-1][...] = total.astype(refs[-1].dtype)


def join(name, *terms):
    return pl.pallas_call(
        join_kernel,
        out_shape=jax.ShapeDtypeStruct(terms[0].shape, jnp.bfloat16),
        compiler_params=params(),
        name=name,
    )(*terms)


def norm_kernel(place, gathered_ref, *refs, parts):
    out_ref = refs[-1]
    blocks = (len(refs) - 1) // parts
    chunk, width = refs[0].shape
    b = place[4]
    for m in range(parts):
        rows = [refs[k * parts + m][...].astype(jnp.float32) for k in range(blocks)]
        mean = sum(jnp.sum(r, axis=-1, keepdims=True) for r in rows) / D
        rows = [r - mean for r in rows]
        variance = sum(jnp.sum(r * r, axis=-1, keepdims=True) for r in rows) / D
        scale = lax.rsqrt(variance + 1e-05)
        for k in range(blocks):
            gain = gathered_ref[b ^ k, chunk : chunk + PAD, :].astype(jnp.float32)[:1]
            out_ref[m * chunk : (m + 1) * chunk, k * width : (k + 1) * width] = (
                rows[k] * scale * gain
            ).astype(jnp.bfloat16)


def norm(place, gathered, columns):
    blocks, parts = len(columns), len(columns[0])
    chunk, width = columns[0][0].shape
    whole = lambda a: pl.BlockSpec(a.shape, lambda i, *_: (0,) * a.ndim)
    flat = [a for column in columns for a in column]
    return pl.pallas_call(
        functools.partial(norm_kernel, parts=parts),
        grid_spec=pltpu.PrefetchScalarGridSpec(
            num_scalar_prefetch=1,
            grid=(1,),
            in_specs=[whole(gathered)] + [whole(a) for a in flat],
            out_specs=pl.BlockSpec((parts * chunk, blocks * width), lambda i, *_: (0, 0)),
        ),
        out_shape=jax.ShapeDtypeStruct((parts * chunk, blocks * width), jnp.bfloat16),
        compiler_params=params(),
        name="norm",
    )(place, gathered, *flat)


def up_kernel(place, rows_ref, hot_ref, out_ref):
    weight = jnp.concatenate([hot_ref[i] for i in range(hot_ref.shape[0])], axis=1)
    out_ref[...] = jnp.dot(
        rows_ref[...], weight, preferred_element_type=jnp.float32
    ).astype(out_ref.dtype)


def up(place, half, normed, hot):
    width = hot.shape[1]
    rows = normed.shape[0]
    per = 2
    steps = hot.shape[0] // (2 * per)
    return pl.pallas_call(
        up_kernel,
        grid_spec=pltpu.PrefetchScalarGridSpec(
            num_scalar_prefetch=1,
            grid=(steps,),
            in_specs=[
                pl.BlockSpec((rows, width), lambda i, *_: (0, 0)),
                pl.BlockSpec(
                    (per, width, HD), lambda i, place: ((place[3] ^ half) * steps + i, 0, 0)
                ),
            ],
            out_specs=pl.BlockSpec((rows, per * HD), lambda i, *_: (0, i)),
        ),
        out_shape=jax.ShapeDtypeStruct((rows, steps * per * HD), jnp.bfloat16),
        compiler_params=params(),
        name="up_keep" if half == 0 else "up_send",
    )(place, normed, hot)


def hidden_kernel(place, counts, rows_ref, lists_ref, up_ref, out_ref, sums, *, parts, steps):
    step = pl.program_id(0)
    total = rows_ref.shape[0]
    chunk = total // parts
    here = chunk // steps

    @pl.when(step == 0)
    def _():
        sums[...] = jnp.zeros_like(sums)

    weight = jnp.concatenate([up_ref[0], up_ref[1]], axis=1)
    sums[...] += jnp.dot(rows_ref[...], weight, preferred_element_type=jnp.float32)

    @pl.when(step == pl.num_programs(0) - 1)
    def _():
        slots = lists_ref.shape[3]
        index = lax.broadcasted_iota(jnp.int32, (total, slots), 0)
        slot = lax.broadcasted_iota(jnp.int32, (total, slots), 1)
        owner = (index // chunk) ^ place[0]
        row = (index // here % steps) * (parts * here) + owner * here + index % here
        for c in range(2):
            hit = (row == lists_ref[0, 0, c : c + 1, :]) & (slot < counts[2 * place[4] + c])
            used = jnp.max(jnp.where(hit, 1.0, 0.0), axis=-1, keepdims=True)
            made = jnp.maximum(sums[:, c * HD : (c + 1) * HD], 0.0) * used
            out_ref[:, c * HD : (c + 1) * HD] = made.astype(out_ref.dtype)


def cold_hidden(place, counts, normed, lists, cold_up, parts, steps):
    rows = normed.shape[0]
    blocks = lists.shape[0]
    width = normed.shape[1] // blocks
    return pl.pallas_call(
        functools.partial(hidden_kernel, parts=parts, steps=steps),
        grid_spec=pltpu.PrefetchScalarGridSpec(
            num_scalar_prefetch=2,
            grid=(blocks,),
            in_specs=[
                pl.BlockSpec((rows, width), lambda i, *_: (0, i)),
                pl.BlockSpec((1,) + lists.shape[1:], lambda i, place, _: (place[4], 0, 0, 0)),
                pl.BlockSpec((2, width, HD), lambda i, place, _: (0, place[4] ^ i, 0)),
            ],
            out_specs=pl.BlockSpec((rows, 2 * HD), lambda i, *_: (0, 0)),
            scratch_shapes=[pltpu.VMEM((rows, 2 * HD), jnp.float32)],
        ),
        out_shape=jax.ShapeDtypeStruct((rows, 2 * HD), jnp.bfloat16),
        compiler_params=params(),
        name="cold_hidden",
    )(place, counts, normed, lists, cold_up)


def piece_kernel(place, hidden_ref, down_ref, out_ref):
    depth, wide = down_ref.shape[1:]
    out_ref[0] = jnp.dot(
        hidden_ref[...],
        down_ref[...].reshape(2 * depth, wide),
        preferred_element_type=jnp.float32,
    ).astype(out_ref.dtype)


def cold_pieces(place, odd, hidden, cold_down, blocks):
    rows = hidden.shape[0]
    width = cold_down.shape[2] // blocks
    return pl.pallas_call(
        piece_kernel,
        grid_spec=pltpu.PrefetchScalarGridSpec(
            num_scalar_prefetch=1,
            grid=(2,),
            in_specs=[
                pl.BlockSpec(hidden.shape, lambda i, *_: (0, 0)),
                pl.BlockSpec((2, HD, width), lambda i, place: (0, 0, place[4] ^ (2 * i + odd))),
            ],
            out_specs=pl.BlockSpec((1, rows, width), lambda i, *_: (i, 0, 0)),
        ),
        out_shape=jax.ShapeDtypeStruct((2, rows, width), jnp.bfloat16),
        compiler_params=params(),
        name="cold_send" if odd else "cold_keep",
    )(place, hidden, cold_down)


def down_kernel(place, hidden_ref, hot_ref, *refs):
    blocks, depth, wide = hot_ref.shape
    made = jnp.dot(
        hidden_ref[...],
        hot_ref[...].reshape(blocks * depth, wide),
        preferred_element_type=jnp.float32,
    )
    for ref in refs[:-1]:
        made = made + (ref[0] if ref.ndim == 3 else ref[...]).astype(jnp.float32)
    refs[-1][...] = made


def down(place, half, hidden, hot, *before):
    rows = hidden.shape[0]
    width = hot.shape[2]
    wide = width // 3
    blocks = hot.shape[0] // 2
    column = lambda i, *_: (0, i)
    return pl.pallas_call(
        down_kernel,
        grid_spec=pltpu.PrefetchScalarGridSpec(
            num_scalar_prefetch=1,
            grid=(width // wide,),
            in_specs=[
                pl.BlockSpec(hidden.shape, lambda i, *_: (0, 0)),
                pl.BlockSpec((blocks, HD, wide), lambda i, place: (place[3] ^ half, 0, i)),
            ]
            + [
                pl.BlockSpec((1, rows, wide), lambda i, *_: (0, 0, i))
                if a.ndim == 3
                else pl.BlockSpec((rows, wide), column)
                for a in before
            ],
            out_specs=pl.BlockSpec((rows, wide), column),
        ),
        out_shape=jax.ShapeDtypeStruct((rows, width), jnp.float32),
        compiler_params=params(),
        name="down_keep" if half == 0 else "down_got",
    )(place, hidden, hot, *before)


def chunks_kernel(base_ref, more_ref, *outs):
    made = base_ref[...] + more_ref[...].astype(jnp.float32)
    chunk = outs[0].shape[0]
    for m, out in enumerate(outs):
        out[...] = made[m * chunk : (m + 1) * chunk].astype(out.dtype)


def into_chunks(base, more, parts):
    rows, width = base.shape
    return pl.pallas_call(
        chunks_kernel,
        out_shape=[
            jax.ShapeDtypeStruct((rows // parts, width), jnp.bfloat16 if m else jnp.float32)
            for m in range(parts)
        ],
        compiler_params=params(),
        name="into_chunks",
    )(base, more)


def swap(x, axis, m, size=4):
    return lax.ppermute(x, axis, [(i, i ^ m) for i in range(size)])


def local_fast(
    queries,
    key_cache,
    value_cache,
    key_new,
    value_new,
    lengths,
    out_proj,
    residual,
    norm_gain,
    hot_up,
    hot_down,
    cold_up,
    cold_down,
    block_rows,
    block_counts,
):
    steps, here, _ = queries.shape
    all_rows, width = residual.shape[1:]
    parts = all_rows // here
    blocks = block_rows.shape[0]
    others = range(1, parts)
    b = lax.axis_index("blocks")
    h = lax.axis_index("heads")
    place = jnp.stack([h, b // 2, b, b % 2, b]).astype(jnp.int32)
    counts = block_counts.reshape(-1)

    gain = norm_gain[None]
    attended = attention(queries, key_cache, value_cache, key_new, value_new, gain, lengths)
    gathered = lax.all_gather(attended, "blocks", axis=0)
    pieces = project(place, gathered, out_proj)
    got = [swap(pieces[m], "heads", m) for m in others]
    mine = lax.dynamic_slice(residual, (0, h * here, 0), (steps, here, width))
    state = join("join", mine.reshape(steps * here, width), pieces[0], *got)
    states = [state] + [swap(state, "heads", m) for m in others]
    across = [swap(s, "blocks", 2) for s in states]
    columns = [
        states,
        [swap(s, "blocks", 1) for s in states],
        across,
        [swap(s, "blocks", 1) for s in across],
    ]
    normed = norm(place, gathered, columns)

    sent = swap(up(place, 1, normed, hot_up), "blocks", 1)
    kept = up(place, 0, normed, hot_up)
    summed = join("join_hot", kept, sent)
    arrived = swap(summed, "blocks", 2)

    cold = cold_hidden(place, counts, normed, block_rows, cold_up, parts, steps)
    cold_got = swap(cold_pieces(place, 1, cold, cold_down, blocks), "blocks", 1)
    cold_kept = cold_pieces(place, 0, cold, cold_down, blocks)
    far = (cold_kept[1].astype(jnp.float32) + cold_got[1].astype(jnp.float32)).astype(jnp.bfloat16)
    cold_far = swap(far, "blocks", 2)

    total = summed.astype(jnp.float32) + arrived.astype(jnp.float32)
    hidden = jnp.maximum(total, 0.0).astype(jnp.bfloat16)
    partner = swap(hidden, "blocks", 1)
    base = down(place, 0, hidden, hot_down)
    base = down(place, 1, partner, hot_down, base, cold_kept, cold_got)
    made = into_chunks(base, cold_far, parts)
    out = made[0]
    for m in others:
        out = out + swap(made[m], "heads", m).astype(jnp.float32)
    ffn_out = out.astype(jnp.bfloat16).reshape(steps, here, width)

    stacked = jnp.stack(states).reshape(parts, steps, 1, here, width)
    ordered = [
        lax.dynamic_index_in_dim(stacked, c ^ h, axis=0, keepdims=False) for c in range(parts)
    ]
    attn_state = jnp.concatenate(ordered, axis=1).reshape(steps, all_rows, width)
    return (attn_state, ffn_out)


def solution(mesh):
    placed = (
        P(None, ("groups", "blocks"), "heads"),
        P(("groups", "blocks"), None, "heads"),
        P(("groups", "blocks"), None, "heads"),
        P(None, ("groups", "blocks"), "heads"),
        P(None, ("groups", "blocks"), "heads"),
        P(("groups", "blocks")),
        P("heads", "blocks"),
        P(None, "groups", "blocks"),
        P("blocks"),
        P("heads", "blocks", None),
        P("heads", None, "blocks"),
        P(("blocks", "heads"), None, None),
        P(("blocks", "heads"), None, None),
        P("groups", "heads", None, None),
        P("groups", "heads", None),
    )
    sizes = tuple(mesh.shape[a] for a in ("blocks", "heads"))
    return jax.shard_map(
        local_fast if sizes == (4, 4) else local,
        mesh=mesh,
        in_specs=placed,
        out_specs=(P(None, "groups", "blocks"), P(None, ("groups", "heads"), "blocks")),
        check_vma=False,
    )
```

```python
import functools
import math

import jax
import jax.numpy as jnp
from jax import lax
from jax.experimental import pallas as pl
from jax.experimental.pallas import tpu as pltpu
from jax.sharding import PartitionSpec as P

HD = 128
D = 6144


def local(
    queries,
    key_cache,
    value_cache,
    key_new,
    value_new,
    lengths,
    out_proj,
    residual,
    norm_gain,
    hot_up,
    hot_down,
    cold_up,
    cold_down,
    block_rows,
    block_counts,
):
    steps, rows_here, width_here = queries.shape
    heads_here = width_here // HD
    context = key_cache.shape[1]
    query_heads = queries.reshape(steps, rows_here, heads_here, HD)
    cached_keys = key_cache.reshape(rows_here, context, heads_here, HD)
    cached_values = value_cache.reshape(rows_here, context, heads_here, HD)
    recent_keys = key_new.reshape(steps, rows_here, heads_here, HD)
    recent_values = value_new.reshape(steps, rows_here, heads_here, HD)
    factor = 1.0 / math.sqrt(HD)
    old_scores = (
        jnp.einsum("trhd,rphd->trhp", query_heads, cached_keys, preferred_element_type=jnp.float32)
        * factor
    )
    visible = jnp.arange(context)[None, :] < lengths[:, None]
    old_scores = jnp.where(visible[None, :, None, :], old_scores, -jnp.inf)
    new_scores = (
        jnp.einsum("trhd,srhd->trhs", query_heads, recent_keys, preferred_element_type=jnp.float32)
        * factor
    )
    causal = jnp.arange(steps)[None, :] <= jnp.arange(steps)[:, None]
    new_scores = jnp.where(causal[:, None, None, :], new_scores, -jnp.inf)
    highest = jnp.maximum(jnp.max(old_scores, axis=-1), jnp.max(new_scores, axis=-1))[..., None]
    old_weights = jnp.exp(old_scores - highest)
    new_weights = jnp.exp(new_scores - highest)
    denominator = jnp.sum(old_weights, axis=-1, keepdims=True) + jnp.sum(
        new_weights, axis=-1, keepdims=True
    )
    old_probs = (old_weights / denominator).astype(jnp.bfloat16)
    new_probs = (new_weights / denominator).astype(jnp.bfloat16)
    attended = jnp.einsum(
        "trhp,rphd->trhd", old_probs, cached_values, preferred_element_type=jnp.float32
    )
    attended = attended + jnp.einsum(
        "trhs,srhd->trhd", new_probs, recent_values, preferred_element_type=jnp.float32
    )
    attended = attended.reshape(steps, rows_here, width_here).astype(jnp.bfloat16)
    partial_out = jnp.einsum(
        "trk,kc->trc",
        lax.all_gather(attended, "blocks", axis=1, tiled=True),
        out_proj,
        preferred_element_type=jnp.float32,
    )
    summed = lax.psum(partial_out.astype(jnp.bfloat16), "heads").astype(jnp.float32)
    state = (residual.astype(jnp.float32) + summed).astype(jnp.bfloat16)
    state_wide = state.astype(jnp.float32)
    mean_row = lax.psum(jnp.sum(state_wide, axis=-1), "blocks") / D
    centred = state_wide - mean_row[..., None]
    variance = lax.psum(jnp.sum(centred * centred, axis=-1), "blocks") / D
    normed = (
        centred * lax.rsqrt(variance + 1e-05)[..., None] * norm_gain.astype(jnp.float32)
    ).astype(jnp.bfloat16)
    hot_inputs = jnp.einsum("trc,kch->trkh", normed, hot_up, preferred_element_type=jnp.float32)
    hot_total = lax.psum(hot_inputs.astype(jnp.bfloat16), "blocks").astype(jnp.float32)
    hot_hidden = jnp.maximum(hot_total, 0.0).astype(jnp.bfloat16)
    hot_sum = jnp.einsum("trkh,khc->trc", hot_hidden, hot_down, preferred_element_type=jnp.float32)
    all_rows = normed.shape[1]
    slice_width = normed.shape[2]
    flat_rows = normed.reshape(steps * all_rows, slice_width)
    slot_rows = block_rows[:, 0]
    slot_counts = block_counts[:, 0]
    outgoing = flat_rows[slot_rows]
    hidden = jnp.maximum(
        jnp.einsum(
            "ocnd,cdh->ocnh",
            lax.all_to_all(outgoing, "blocks", split_axis=0, concat_axis=3, tiled=True),
            cold_up,
            preferred_element_type=jnp.float32,
        ),
        0.0,
    ).astype(jnp.bfloat16)
    made = jnp.einsum(
        "ocnh,chd->ocnd", hidden, cold_down, preferred_element_type=jnp.float32
    ).astype(jnp.bfloat16)
    returned = lax.all_to_all(made, "blocks", split_axis=3, concat_axis=0, tiled=True)
    keep = jnp.arange(returned.shape[2])[None, None, :] < slot_counts[..., None]
    gained = jnp.where(keep[..., None], returned.astype(jnp.float32), 0.0)
    cold_sum = (
        jnp.zeros((steps * all_rows, slice_width), jnp.float32)
        .at[slot_rows.reshape(-1)]
        .add(gained.reshape(-1, slice_width))
    )
    total = cold_sum.reshape(steps, all_rows, slice_width) + hot_sum
    ffn_out = lax.psum_scatter(total.astype(jnp.bfloat16), "heads", scatter_dimension=1, tiled=True)
    return (state, ffn_out)


VMEM = pl.BlockSpec(memory_space=pltpu.VMEM)
SMEM = pl.BlockSpec(memory_space=pltpu.SMEM)
AWAY = pl.BlockSpec(memory_space=pl.ANY)
DMA = pltpu.SemaphoreType.DMA


COSTS = {"cold_send": 60, "cold_keep": 10, "down_keep": 10, "down_got": 10}
LIMITS = {
    "attention": 123,
    "project": 120,
    "norm_up_send": 116,
    "up_keep": 116,
    "cold_send": 121,
    "cold_keep": 121,
    "down_keep": 116,
    "down_got": 116,
}


def call(kernel, name, out_shape, specs, operands, scratch=()):
    return pl.pallas_call(
        kernel,
        in_specs=specs,
        out_specs=jax.tree.map(lambda _: VMEM, out_shape),
        out_shape=out_shape,
        scratch_shapes=list(scratch),
        compiler_params=pltpu.CompilerParams(vmem_limit_bytes=LIMITS.get(name, 32) * 2**19),
        cost_estimate=pl.CostEstimate(
            flops=0, bytes_accessed=COSTS.get(name, 6) * 10**6, transcendentals=0
        ),
        name=name,
    )(*operands)


def begin(copies):
    for copy in copies:
        copy.start()


def finish(copies):
    for copy in copies:
        copy.wait()


def like(rows, width, dtype=jnp.bfloat16):
    return jax.ShapeDtypeStruct((rows, width), dtype)


def attention_kernel(
    lengths, q, kn, vn, keys, values, out_ref, small, key_buf, value_buf, small_sems, sems, *, here, steps
):
    rows, width = q.shape
    context = keys.shape[0] // here
    wide = 2 * HD
    parts = wide // HD
    count = width // wide

    def copies(i):
        column = pl.ds(i * wide, wide)
        return (
            pltpu.make_async_copy(keys.at[:, column], key_buf.at[i], sems.at[0, i]),
            pltpu.make_async_copy(values.at[:, column], value_buf.at[i], sems.at[1, i]),
        )

    heads = [
        pltpu.make_async_copy(ref, small.at[i], small_sems.at[i]) for i, ref in enumerate((q, kn, vn))
    ]
    begin(heads)
    for i in range(count):
        begin(copies(i))
    q_ref, kn_ref, vn_ref = small.at[0], small.at[1], small.at[2]

    nt = (((1,), (1,)), ((), ()))
    factor = 1.0 / math.sqrt(HD)
    lane_head = lax.broadcasted_iota(jnp.int32, (rows, wide), 1) // HD
    row = lax.broadcasted_iota(jnp.int32, (parts * rows, context), 0) % here
    slot = lax.broadcasted_iota(jnp.int32, (parts * rows, context), 1)
    limit = jnp.zeros_like(slot)
    for r in range(here):
        limit = jnp.where(row == r, lengths[r], limit)
    open_slot = slot < limit
    at = lax.broadcasted_iota(jnp.int32, (parts * rows, rows), 0) % rows
    to = lax.broadcasted_iota(jnp.int32, (parts * rows, rows), 1)
    seen = (at % here == to % here) & (to // here <= at // here)
    finish(heads)
    for i in range(count):
        column = slice(i * wide, (i + 1) * wide)
        q = q_ref[:, column]
        split = jnp.concatenate(
            [jnp.where(lane_head == j, q, jnp.zeros_like(q)) for j in range(parts)], axis=0
        )
        fresh = lax.dot_general(split, kn_ref[:, column], nt, preferred_element_type=jnp.float32)
        fresh = jnp.where(seen, fresh * factor, -jnp.inf)
        key_copy, value_copy = copies(i)
        key_copy.wait()
        scores = lax.dot_general(split, key_buf[i], nt, preferred_element_type=jnp.float32)
        own = scores[:, :context]
        for r in range(1, here):
            own = jnp.where(row == r, scores[:, r * context : (r + 1) * context], own)
        own = jnp.where(open_slot, own * factor, -jnp.inf)
        top = jnp.maximum(
            jnp.max(own, axis=-1, keepdims=True), jnp.max(fresh, axis=-1, keepdims=True)
        )
        own = jnp.exp(own - top)
        fresh = jnp.exp(fresh - top)
        scale = 1.0 / (
            jnp.sum(own, axis=-1, keepdims=True) + jnp.sum(fresh, axis=-1, keepdims=True)
        )
        own = own * scale
        spread = jnp.concatenate(
            [jnp.where(row == r, own, 0.0).astype(jnp.bfloat16) for r in range(here)], axis=1
        )
        value_copy.wait()
        got = jnp.dot(spread, value_buf[i], preferred_element_type=jnp.float32)
        got = got + jnp.dot(
            (fresh * scale).astype(jnp.bfloat16),
            vn_ref[:, column],
            preferred_element_type=jnp.float32,
        )
        answer = got[:rows]
        for j in range(1, parts):
            answer = jnp.where(lane_head == j, got[j * rows : (j + 1) * rows], answer)
        out_ref[:, column] = answer.astype(jnp.bfloat16)


def attention(queries, key_cache, value_cache, key_new, value_new, lengths):
    steps, here, width = queries.shape
    slots = here * key_cache.shape[1]
    count = width // (2 * HD)
    flat = lambda a: a.reshape(-1, width)
    return call(
        functools.partial(attention_kernel, here=here, steps=steps),
        "attention",
        like(steps * here, width),
        [SMEM] + [AWAY] * 5,
        (
            lengths,
            flat(queries),
            flat(key_new),
            flat(value_new),
            flat(key_cache),
            flat(value_cache),
        ),
        [
            pltpu.VMEM((3, steps * here, width), jnp.bfloat16),
            pltpu.VMEM((count, slots, 2 * HD), jnp.bfloat16),
            pltpu.VMEM((count, slots, 2 * HD), jnp.bfloat16),
            DMA((3,)),
            DMA((2, count)),
        ],
    )


def project_kernel(place, *refs, parts):
    rows_refs, weight, outs = refs[:parts], refs[parts], refs[parts + 1 : -4]
    held, weight_buf, total, sems = refs[-4:]
    chunk = outs[0].shape[0]
    depth = weight.shape[0]
    count = 6
    deep = depth // count
    copies = [
        pltpu.make_async_copy(
            weight.at[pl.ds(i * deep, deep)], weight_buf.at[pl.ds(i * deep, deep)], sems.at[i]
        )
        for i in range(count)
    ]
    begin(copies)
    for k, ref in enumerate(rows_refs):
        held[k] = ref[...]
    rows = jnp.concatenate([held[place[0] ^ place[1] ^ m] for m in range(parts)], axis=0)
    for i in range(0, count, 2):
        finish(copies[i : i + 2])
        span = slice(i * deep, (i + 2) * deep)
        made = jnp.dot(rows[:, span], weight_buf[span], preferred_element_type=jnp.float32)
        if i:
            made = made + total[...]
        if i + 2 < count:
            total[...] = made
    for m, out in enumerate(outs):
        out[...] = made[m * chunk : (m + 1) * chunk].astype(out.dtype)


def project(place, gathered, weight):
    parts = len(gathered)
    chunk, depth = gathered[0].shape
    width = weight.shape[1]
    return call(
        functools.partial(project_kernel, parts=parts),
        "project",
        [like(chunk, width, jnp.bfloat16 if m else jnp.float32) for m in range(parts)],
        [SMEM] + [VMEM] * parts + [AWAY],
        (place, *gathered, weight),
        [
            pltpu.VMEM((parts, chunk, depth), jnp.bfloat16),
            pltpu.VMEM(weight.shape, jnp.bfloat16),
            pltpu.VMEM((parts * chunk, width), jnp.float32),
            DMA((6,)),
        ],
    )


def join_kernel(*refs, terms):
    total = refs[0][...].astype(jnp.float32)
    for ref in refs[1:terms]:
        total = total + ref[...].astype(jnp.float32)
    refs[-1][...] = total.astype(refs[-1].dtype)


def join(name, terms, after=()):
    return call(
        functools.partial(join_kernel, terms=len(terms)),
        name,
        like(*terms[0].shape),
        [VMEM] * (len(terms) + len(after)),
        (*terms, *after),
    )


def norm_kernel(place, gain_ref, hot, *refs, parts, blocks):
    states, (sent_ref, own_ref, stat_ref, buf, sems) = refs[:-5], refs[-5:]
    copies = half_copies(hot, place[2] ^ 1, buf, sems)
    begin(copies)
    chunk, width = states[0].shape
    gain = gain_ref[...].astype(jnp.float32)
    for m in range(parts):
        place_rows = slice(m * chunk, (m + 1) * chunk)
        rows = [states[k * parts + m][...].astype(jnp.float32) for k in range(blocks)]
        total = rows[0]
        for r in rows[1:]:
            total = total + r
        mean = jnp.sum(total, axis=-1, keepdims=True) / D
        rows = [r - mean for r in rows]
        total = rows[0] * rows[0]
        for r in rows[1:]:
            total = total + r * r
        variance = jnp.sum(total, axis=-1, keepdims=True) / D
        scale = lax.rsqrt(variance + 1e-05)
        own_ref[place_rows, :] = (rows[0] * scale * gain).astype(jnp.bfloat16)
        stat_ref[0, place_rows, :] = jnp.broadcast_to(mean, (chunk, HD))
        stat_ref[1, place_rows, :] = jnp.broadcast_to(scale, (chunk, HD))
    up_half(own_ref, copies, buf, sent_ref)


def half_copies(hot, half, buf, sems):
    count = buf.shape[0]
    return [
        pltpu.make_async_copy(
            hot.at[pl.ds(half * count + i, 2)], buf.at[pl.ds(i, 2)], sems.at[i // 2]
        )
        for i in range(0, count, 2)
    ]


def half_scratch(hot):
    count = hot.shape[0] // 2
    return [pltpu.VMEM((count,) + hot.shape[1:], jnp.bfloat16), DMA((count // 2,))]


def up_half(rows_ref, copies, buf, out_ref):
    rows = rows_ref[...]
    for i, copy in enumerate(copies):
        copy.wait()
        weight = jnp.concatenate([buf[2 * i], buf[2 * i + 1]], axis=1)
        out_ref[:, 2 * i * HD : 2 * (i + 1) * HD] = jnp.dot(
            rows, weight, preferred_element_type=jnp.float32
        ).astype(out_ref.dtype)


def norm(place, gain, hot, columns):
    blocks, parts = len(columns), len(columns[0])
    chunk, width = columns[0][0].shape
    rows = parts * chunk
    return call(
        functools.partial(norm_kernel, parts=parts, blocks=blocks),
        "norm_up_send",
        [
            like(rows, hot.shape[0] // 2 * HD),
            like(rows, width),
            jax.ShapeDtypeStruct((2, rows, HD), jnp.float32),
        ],
        [SMEM, VMEM, AWAY] + [VMEM] * (blocks * parts),
        (place, gain, hot, *[a for column in columns for a in column]),
        half_scratch(hot),
    )


def up_kernel(place, rows_ref, hot, out_ref, buf, sems):
    copies = half_copies(hot, place[2], buf, sems)
    begin(copies)
    up_half(rows_ref, copies, buf, out_ref)


def up_keep(place, rows, hot):
    return call(
        up_kernel,
        "up_keep",
        like(rows.shape[0], hot.shape[0] // 2 * HD),
        [SMEM, VMEM, AWAY],
        (place, rows, hot),
        half_scratch(hot),
    )


def piece_copies(cold_down, block, width, buf, i, sems):
    at = pl.ds(pl.multiple_of(block * width, width), width)
    return [
        pltpu.make_async_copy(cold_down.at[c, :, at], buf.at[i, c], sems.at[i, c]) for c in range(2)
    ]


def piece_scratch(cold_down, width):
    return [pltpu.VMEM((2, 2, cold_down.shape[1], width), jnp.bfloat16), DMA((2, 2))]


def piece(hidden, copies, buf, i):
    finish(copies)
    depth, width = buf.shape[2:]
    return jnp.dot(
        hidden, buf[i].reshape(2 * depth, width), preferred_element_type=jnp.float32
    ).astype(jnp.bfloat16)


def cold_kernel(place, counts, lists_ref, stat_ref, after, up, down, *refs, parts, steps):
    blocks = lists_ref.shape[0]
    gains, states = refs[:blocks], refs[blocks:-6]
    hidden_ref, out_ref, up_buf, up_sems, down_buf, down_sems = refs[-6:]
    chunk, width = states[0].shape
    total = parts * chunk
    here = chunk // steps
    b = place[1]
    up_copies = [
        [
            pltpu.make_async_copy(
                up.at[c, pl.ds(pl.multiple_of((b ^ k) * width, width), width)],
                up_buf.at[k, c],
                up_sems.at[k, c],
            )
            for c in range(2)
        ]
        for k in range(blocks)
    ]
    down_copies = [
        piece_copies(down, b ^ (2 * i + 1), width, down_buf, i, down_sems) for i in range(2)
    ]
    for copies in up_copies + down_copies:
        begin(copies)
    mean, scale = stat_ref[0][:, :1], stat_ref[1][:, :1]
    sums = jnp.zeros((total, 2 * HD), jnp.float32)
    for k in range(blocks):
        rows = jnp.concatenate(
            [states[k * parts + m][...] for m in range(parts)], axis=0
        ).astype(jnp.float32)
        gain = gains[k][...].astype(jnp.float32)
        normed = ((rows - mean) * scale * gain).astype(jnp.bfloat16)
        finish(up_copies[k])
        weight = jnp.concatenate([up_buf[k, 0], up_buf[k, 1]], axis=1)
        sums = sums + jnp.dot(normed, weight, preferred_element_type=jnp.float32)
    slots = lists_ref.shape[3]
    index = lax.broadcasted_iota(jnp.int32, (total, slots), 0)
    slot = lax.broadcasted_iota(jnp.int32, (total, slots), 1)
    owner = (index // chunk) ^ place[0]
    row = (index // here % steps) * (parts * here) + owner * here + index % here
    halves = []
    for c in range(2):
        hit = (row == lists_ref[b, 0, c : c + 1, :]) & (slot < counts[2 * b + c])
        used = jnp.max(jnp.where(hit, 1.0, 0.0), axis=-1, keepdims=True)
        halves.append((jnp.maximum(sums[:, c * HD : (c + 1) * HD], 0.0) * used))
    hidden = jnp.concatenate(halves, axis=1).astype(jnp.bfloat16)
    hidden_ref[...] = hidden
    for i in range(2):
        out_ref[i] = piece(hidden, down_copies[i], down_buf, i)


def cold_send(place, counts, lists, stat, after, cold_up, cold_down, gains, columns, steps):
    blocks, parts = len(columns), len(columns[0])
    chunk, width = columns[0][0].shape
    rows = parts * chunk
    flat = [a for column in columns for a in column]
    return call(
        functools.partial(cold_kernel, parts=parts, steps=steps),
        "cold_send",
        [like(rows, 2 * HD), jax.ShapeDtypeStruct((blocks // 2, rows, width), jnp.bfloat16)],
        [SMEM, SMEM, VMEM, VMEM, AWAY, AWAY, AWAY] + [VMEM] * (blocks + len(flat)),
        (place, counts, lists, stat, after, cold_up, cold_down, *gains, *flat),
        [pltpu.VMEM((blocks, 2, width, HD), jnp.bfloat16), DMA((blocks, 2))]
        + piece_scratch(cold_down, width),
    )


def keep_kernel(place, hidden_ref, down, after, near_ref, far_ref, buf, sems):
    width = near_ref.shape[1]
    copies = [piece_copies(down, place[1] ^ (2 * i), width, buf, i, sems) for i in range(2)]
    begin(copies[1] + copies[0])
    hidden = hidden_ref[...]
    far_ref[...] = piece(hidden, copies[1], buf, 1)
    near_ref[...] = piece(hidden, copies[0], buf, 0)


def cold_keep(place, hidden, cold_down, after, width):
    rows = hidden.shape[0]
    return call(
        keep_kernel,
        "cold_keep",
        [like(rows, width), like(rows, width)],
        [SMEM, VMEM, AWAY, AWAY],
        (place, hidden, cold_down, after),
        piece_scratch(cold_down, width),
    )


def down_kernel(place, hidden_ref, hot, *refs, half):
    before, (out_ref, buf, sems) = refs[:-3], refs[-3:]
    copies = half_copies(hot, place[2] ^ half, buf, sems)
    begin(copies)
    depth, width = buf.shape[1:]
    for i in range(0, len(copies), 2):
        finish(copies[i : i + 2])
        made = jnp.dot(
            hidden_ref[:, 2 * i * depth : 2 * (i + 2) * depth],
            buf[2 * i : 2 * (i + 2)].reshape(4 * depth, width),
            preferred_element_type=jnp.float32,
        )
        if i:
            made = made + out_ref[...]
        else:
            for ref in before:
                made = made + ref[...].astype(jnp.float32)
        out_ref[...] = made


def down(place, half, hidden, hot, *before):
    return call(
        functools.partial(down_kernel, half=half),
        "down_got" if half else "down_keep",
        like(hidden.shape[0], hot.shape[2], jnp.float32),
        [SMEM, VMEM, AWAY] + [VMEM] * len(before),
        (place, hidden, hot, *before),
        half_scratch(hot),
    )


def chunks_kernel(base_ref, more_ref, *outs):
    chunk = outs[0].shape[0]
    for m, out in enumerate(outs):
        rows = slice(m * chunk, (m + 1) * chunk)
        out[...] = (base_ref[rows, :] + more_ref[rows, :].astype(jnp.float32)).astype(out.dtype)


def into_chunks(base, more, parts):
    rows, width = base.shape
    return call(
        chunks_kernel,
        "into_chunks",
        [like(rows // parts, width, jnp.bfloat16 if m else jnp.float32) for m in range(parts)],
        [VMEM, VMEM],
        (base, more),
    )


def swap(x, axis, m, size=4):
    return lax.ppermute(x, axis, [(i, i ^ m) for i in range(size)])


def local_fast(
    queries,
    key_cache,
    value_cache,
    key_new,
    value_new,
    lengths,
    out_proj,
    residual,
    norm_gain,
    hot_up,
    hot_down,
    cold_up,
    cold_down,
    block_rows,
    block_counts,
):
    steps, here, _ = queries.shape
    all_rows, width = residual.shape[1:]
    parts = all_rows // here
    blocks = block_rows.shape[0]
    others = range(1, parts)
    b = lax.axis_index("blocks")
    h = lax.axis_index("heads")
    place = jnp.stack([h, b, b % 2]).astype(jnp.int32)
    counts = block_counts.reshape(-1)

    attended = attention(queries, key_cache, value_cache, key_new, value_new, lengths)
    across = swap(attended, "blocks", 2)
    gathered = [attended, swap(attended, "blocks", 1), across, swap(across, "blocks", 1)]
    pieces = project(place, gathered, out_proj)
    got = [swap(pieces[m], "heads", m) for m in others]
    gain = norm_gain[None]
    gains = [gain] + [swap(gain, "blocks", k) for k in range(1, blocks)]
    mine = lax.dynamic_slice(residual, (0, h * here, 0), (steps, here, width))
    state = join("join", [mine.reshape(steps * here, width), pieces[0], *got], gains[1:])
    states = [state] + [swap(state, "heads", m) for m in others]
    across = [swap(s, "blocks", 2) for s in states]
    columns = [
        states,
        [swap(s, "blocks", 1) for s in states],
        across,
        [swap(s, "blocks", 1) for s in across],
    ]
    sent, own, stat = norm(place, gain, hot_up, columns)
    sent = swap(sent, "blocks", 1)
    kept = up_keep(place, own, hot_up)
    summed = join("join_hot", [kept, sent])
    arrived = swap(summed, "blocks", 2)

    cold, cold_sent = cold_send(
        place, counts, block_rows, stat, summed, cold_up, cold_down, gains, columns, steps
    )
    cold_sent, arrived = lax.optimization_barrier((cold_sent, arrived))
    cold_got = swap(cold_sent, "blocks", 1)
    total = summed.astype(jnp.float32) + arrived.astype(jnp.float32)
    hidden = jnp.maximum(total, 0.0).astype(jnp.bfloat16)
    near, far = cold_keep(place, cold, cold_down, hidden, width)
    far = (far.astype(jnp.float32) + cold_got[1].astype(jnp.float32)).astype(jnp.bfloat16)
    cold_far = swap(far, "blocks", 2)
    partner = swap(hidden, "blocks", 1)
    base = down(place, 0, hidden, hot_down)
    base = down(place, 1, partner, hot_down, base, near, cold_got[0])
    made = into_chunks(base, cold_far, parts)
    out = made[0]
    for m in others:
        out = out + swap(made[m], "heads", m).astype(jnp.float32)
    ffn_out = out.astype(jnp.bfloat16).reshape(steps, here, width)

    stacked = jnp.stack(states).reshape(parts, steps, 1, here, width)
    ordered = [
        lax.dynamic_index_in_dim(stacked, c ^ h, axis=0, keepdims=False) for c in range(parts)
    ]
    attn_state = jnp.concatenate(ordered, axis=1).reshape(steps, all_rows, width)
    return (attn_state, ffn_out)


def solution(mesh):
    placed = (
        P(None, ("groups", "blocks"), "heads"),
        P(("groups", "blocks"), None, "heads"),
        P(("groups", "blocks"), None, "heads"),
        P(None, ("groups", "blocks"), "heads"),
        P(None, ("groups", "blocks"), "heads"),
        P(("groups", "blocks")),
        P("heads", "blocks"),
        P(None, "groups", "blocks"),
        P("blocks"),
        P("heads", "blocks", None),
        P("heads", None, "blocks"),
        P(("blocks", "heads"), None, None),
        P(("blocks", "heads"), None, None),
        P("groups", "heads", None, None),
        P("groups", "heads", None),
    )
    sizes = tuple(mesh.shape[a] for a in ("blocks", "heads"))
    return jax.shard_map(
        local_fast if sizes == (4, 4) else local,
        mesh=mesh,
        in_specs=placed,
        out_specs=(P(None, "groups", "blocks"), P(None, ("groups", "heads"), "blocks")),
        check_vma=False,
    )
```

```python
import functools
import math

import jax
import jax.numpy as jnp
from jax import lax
from jax.experimental import pallas as pl
from jax.experimental.pallas import tpu as pltpu
from jax.sharding import PartitionSpec as P

HD = 128
D = 6144


def local(
    queries,
    key_cache,
    value_cache,
    key_new,
    value_new,
    lengths,
    out_proj,
    residual,
    norm_gain,
    hot_up,
    hot_down,
    cold_up,
    cold_down,
    block_rows,
    block_counts,
):
    steps, rows_here, width_here = queries.shape
    heads_here = width_here // HD
    context = key_cache.shape[1]
    query_heads = queries.reshape(steps, rows_here, heads_here, HD)
    cached_keys = key_cache.reshape(rows_here, context, heads_here, HD)
    cached_values = value_cache.reshape(rows_here, context, heads_here, HD)
    recent_keys = key_new.reshape(steps, rows_here, heads_here, HD)
    recent_values = value_new.reshape(steps, rows_here, heads_here, HD)
    factor = 1.0 / math.sqrt(HD)
    old_scores = (
        jnp.einsum("trhd,rphd->trhp", query_heads, cached_keys, preferred_element_type=jnp.float32)
        * factor
    )
    visible = jnp.arange(context)[None, :] < lengths[:, None]
    old_scores = jnp.where(visible[None, :, None, :], old_scores, -jnp.inf)
    new_scores = (
        jnp.einsum("trhd,srhd->trhs", query_heads, recent_keys, preferred_element_type=jnp.float32)
        * factor
    )
    causal = jnp.arange(steps)[None, :] <= jnp.arange(steps)[:, None]
    new_scores = jnp.where(causal[:, None, None, :], new_scores, -jnp.inf)
    highest = jnp.maximum(jnp.max(old_scores, axis=-1), jnp.max(new_scores, axis=-1))[..., None]
    old_weights = jnp.exp(old_scores - highest)
    new_weights = jnp.exp(new_scores - highest)
    denominator = jnp.sum(old_weights, axis=-1, keepdims=True) + jnp.sum(
        new_weights, axis=-1, keepdims=True
    )
    old_probs = (old_weights / denominator).astype(jnp.bfloat16)
    new_probs = (new_weights / denominator).astype(jnp.bfloat16)
    attended = jnp.einsum(
        "trhp,rphd->trhd", old_probs, cached_values, preferred_element_type=jnp.float32
    )
    attended = attended + jnp.einsum(
        "trhs,srhd->trhd", new_probs, recent_values, preferred_element_type=jnp.float32
    )
    attended = attended.reshape(steps, rows_here, width_here).astype(jnp.bfloat16)
    partial_out = jnp.einsum(
        "trk,kc->trc",
        lax.all_gather(attended, "blocks", axis=1, tiled=True),
        out_proj,
        preferred_element_type=jnp.float32,
    )
    summed = lax.psum(partial_out.astype(jnp.bfloat16), "heads").astype(jnp.float32)
    state = (residual.astype(jnp.float32) + summed).astype(jnp.bfloat16)
    state_wide = state.astype(jnp.float32)
    mean_row = lax.psum(jnp.sum(state_wide, axis=-1), "blocks") / D
    centred = state_wide - mean_row[..., None]
    variance = lax.psum(jnp.sum(centred * centred, axis=-1), "blocks") / D
    normed = (
        centred * lax.rsqrt(variance + 1e-05)[..., None] * norm_gain.astype(jnp.float32)
    ).astype(jnp.bfloat16)
    hot_inputs = jnp.einsum("trc,kch->trkh", normed, hot_up, preferred_element_type=jnp.float32)
    hot_total = lax.psum(hot_inputs.astype(jnp.bfloat16), "blocks").astype(jnp.float32)
    hot_hidden = jnp.maximum(hot_total, 0.0).astype(jnp.bfloat16)
    hot_sum = jnp.einsum("trkh,khc->trc", hot_hidden, hot_down, preferred_element_type=jnp.float32)
    all_rows = normed.shape[1]
    slice_width = normed.shape[2]
    flat_rows = normed.reshape(steps * all_rows, slice_width)
    slot_rows = block_rows[:, 0]
    slot_counts = block_counts[:, 0]
    outgoing = flat_rows[slot_rows]
    hidden = jnp.maximum(
        jnp.einsum(
            "ocnd,cdh->ocnh",
            lax.all_to_all(outgoing, "blocks", split_axis=0, concat_axis=3, tiled=True),
            cold_up,
            preferred_element_type=jnp.float32,
        ),
        0.0,
    ).astype(jnp.bfloat16)
    made = jnp.einsum(
        "ocnh,chd->ocnd", hidden, cold_down, preferred_element_type=jnp.float32
    ).astype(jnp.bfloat16)
    returned = lax.all_to_all(made, "blocks", split_axis=3, concat_axis=0, tiled=True)
    keep = jnp.arange(returned.shape[2])[None, None, :] < slot_counts[..., None]
    gained = jnp.where(keep[..., None], returned.astype(jnp.float32), 0.0)
    cold_sum = (
        jnp.zeros((steps * all_rows, slice_width), jnp.float32)
        .at[slot_rows.reshape(-1)]
        .add(gained.reshape(-1, slice_width))
    )
    total = cold_sum.reshape(steps, all_rows, slice_width) + hot_sum
    ffn_out = lax.psum_scatter(total.astype(jnp.bfloat16), "heads", scatter_dimension=1, tiled=True)
    return (state, ffn_out)


VMEM = pl.BlockSpec(memory_space=pltpu.VMEM)
SMEM = pl.BlockSpec(memory_space=pltpu.SMEM)
AWAY = pl.BlockSpec(memory_space=pl.ANY)
DMA = pltpu.SemaphoreType.DMA
COSTS = {"join": 60, "attention": 20, "norm_up_send": 20, "up_keep": 20, "cold_send": 30, "cold_keep": 10, "down_keep": 0, "down_got": 0}
LIMITS = {"attention": 123, "load_project": 100, "load_up": 88, "load_cold": 72, "load_down": 84}


def call(kernel, name, out_shape, specs, operands, scratch=()):
    return pl.pallas_call(
        kernel,
        in_specs=specs,
        out_specs=jax.tree.map(lambda _: VMEM, out_shape),
        out_shape=out_shape,
        scratch_shapes=list(scratch),
        compiler_params=pltpu.CompilerParams(vmem_limit_bytes=LIMITS.get(name, 24) * 2**19),
        cost_estimate=pl.CostEstimate(
            flops=0, bytes_accessed=COSTS.get(name, 10) * 10**6, transcendentals=0
        ),
        name=name,
    )(*operands)


def begin(copies):
    for copy in copies:
        copy.start()


def finish(copies):
    for copy in copies:
        copy.wait()


def like(rows, width, dtype=jnp.bfloat16):
    return jax.ShapeDtypeStruct((rows, width), dtype)


def load_kernel(after, *refs):
    count = (len(refs) - 1) // 2
    copies = [
        pltpu.make_async_copy(source, target, refs[-1].at[i])
        for i, (source, target) in enumerate(zip(refs[:count], refs[count:-1]))
    ]
    begin(copies)
    finish(copies)


def load(name, after, *arrays):
    return call(
        load_kernel,
        name,
        [jax.ShapeDtypeStruct(a.shape, a.dtype) for a in arrays],
        [AWAY] * (1 + len(arrays)),
        (after, *arrays),
        [DMA((len(arrays),))],
    )


def attention_kernel(
    lengths, q, kn, vn, keys, values, out_ref, small, key_buf, value_buf, own_buf, prob_buf, sum_buf,
    small_sems, sems, *, here, steps,
):
    rows, width = q.shape
    context = keys.shape[0] // here
    wide = 2 * HD
    parts = wide // HD
    count = width // wide
    step_rows = 2
    deep = step_rows * context
    turns = here // step_rows
    heads = [
        pltpu.make_async_copy(ref, small.at[i], small_sems.at[i]) for i, ref in enumerate((q, kn, vn))
    ]
    key_copies, value_copies = (
        [
            pltpu.make_async_copy(
                ref.at[pl.ds(j * deep, deep)], buf.at[pl.ds(j * deep, deep)], sems.at[which, j]
            )
            for j in range(turns)
        ]
        for which, (ref, buf) in enumerate(((keys, key_buf), (values, value_buf)))
    )
    begin(heads + key_copies + value_copies)

    nt = (((1,), (1,)), ((), ()))
    factor = 1.0 / math.sqrt(HD)
    lane_head = lax.broadcasted_iota(jnp.int32, (rows, wide), 1) // HD
    row = lax.broadcasted_iota(jnp.int32, (parts * rows, context), 0) % here
    slot = lax.broadcasted_iota(jnp.int32, (parts * rows, context), 1)
    limit = jnp.zeros_like(slot)
    for r in range(here):
        limit = jnp.where(row == r, lengths[r], limit)
    open_slot = slot < limit
    at = lax.broadcasted_iota(jnp.int32, (parts * rows, rows), 0) % rows
    to = lax.broadcasted_iota(jnp.int32, (parts * rows, rows), 1)
    seen = (at % here == to % here) & (to // here <= at // here)
    columns = [slice(i * wide, (i + 1) * wide) for i in range(count)]
    finish(heads)
    splits = []
    for column in columns:
        mine = small[0, :, column]
        splits.append(
            jnp.concatenate(
                [jnp.where(lane_head == j, mine, jnp.zeros_like(mine)) for j in range(parts)], axis=0
            )
        )
    for j in range(turns):
        key_copies[j].wait()
        for i, column in enumerate(columns):
            scores = lax.dot_general(
                splits[i],
                key_buf[j * deep : (j + 1) * deep, column],
                nt,
                preferred_element_type=jnp.float32,
            )
            own = own_buf[i] if j else scores[:, :context]
            for r in range(step_rows):
                own = jnp.where(
                    row == j * step_rows + r, scores[:, r * context : (r + 1) * context], own
                )
            own_buf[i] = own
    for i, column in enumerate(columns):
        fresh = lax.dot_general(
            splits[i], small[1, :, column], nt, preferred_element_type=jnp.float32
        )
        fresh = jnp.where(seen, fresh * factor, -jnp.inf)
        own = jnp.where(open_slot, own_buf[i] * factor, -jnp.inf)
        top = jnp.maximum(
            jnp.max(own, axis=-1, keepdims=True), jnp.max(fresh, axis=-1, keepdims=True)
        )
        own = jnp.exp(own - top)
        fresh = jnp.exp(fresh - top)
        scale = 1.0 / (
            jnp.sum(own, axis=-1, keepdims=True) + jnp.sum(fresh, axis=-1, keepdims=True)
        )
        prob_buf[i] = own * scale
        sum_buf[i] = jnp.dot(
            (fresh * scale).astype(jnp.bfloat16),
            small[2, :, column],
            preferred_element_type=jnp.float32,
        )
    for j in range(turns):
        value_copies[j].wait()
        for i, column in enumerate(columns):
            probs = prob_buf[i]
            spread = jnp.concatenate(
                [
                    jnp.where(row == j * step_rows + r, probs, 0.0).astype(jnp.bfloat16)
                    for r in range(step_rows)
                ],
                axis=1,
            )
            got = sum_buf[i] + jnp.dot(
                spread,
                value_buf[j * deep : (j + 1) * deep, column],
                preferred_element_type=jnp.float32,
            )
            if j + 1 < turns:
                sum_buf[i] = got
            else:
                answer = got[:rows]
                for p in range(1, parts):
                    answer = jnp.where(lane_head == p, got[p * rows : (p + 1) * rows], answer)
                out_ref[:, column] = answer.astype(jnp.bfloat16)


def attention(queries, key_cache, value_cache, key_new, value_new, lengths):
    steps, here, width = queries.shape
    context = key_cache.shape[1]
    rows = steps * here
    count = width // (2 * HD)
    flat = lambda a: a.reshape(-1, width)
    return call(
        functools.partial(attention_kernel, here=here, steps=steps),
        "attention",
        like(rows, width),
        [SMEM] + [AWAY] * 5,
        (
            lengths,
            flat(queries),
            flat(key_new),
            flat(value_new),
            flat(key_cache),
            flat(value_cache),
        ),
        [
            pltpu.VMEM((3, rows, width), jnp.bfloat16),
            pltpu.VMEM((here * context, width), jnp.bfloat16),
            pltpu.VMEM((here * context, width), jnp.bfloat16),
            pltpu.VMEM((count, 2 * rows, context), jnp.float32),
            pltpu.VMEM((count, 2 * rows, context), jnp.float32),
            pltpu.VMEM((count, 2 * rows, 2 * HD), jnp.float32),
            DMA((3,)),
            DMA((2, here // 2)),
        ],
    )


def project_kernel(place, *refs, parts):
    rows_refs, weight_ref, outs, held = refs[:parts], refs[parts], refs[parts + 1 : -1], refs[-1]
    chunk = outs[0].shape[0]
    for k, ref in enumerate(rows_refs):
        held[k] = ref[...]
    rows = jnp.concatenate([held[place[0] ^ place[1] ^ m] for m in range(parts)], axis=0)
    width = weight_ref.shape[1]
    wide = width // 3
    for i in range(3):
        column = slice(i * wide, (i + 1) * wide)
        made = jnp.dot(rows, weight_ref[:, column], preferred_element_type=jnp.float32)
        for m, out in enumerate(outs):
            out[:, column] = made[m * chunk : (m + 1) * chunk].astype(out.dtype)


def project(place, gathered, weight):
    parts = len(gathered)
    chunk, depth = gathered[0].shape
    width = weight.shape[1]
    return call(
        functools.partial(project_kernel, parts=parts),
        "project",
        [like(chunk, width, jnp.bfloat16 if m else jnp.float32) for m in range(parts)],
        [SMEM] + [VMEM] * (parts + 1),
        (place, *gathered, weight),
        [pltpu.VMEM((parts, chunk, depth), jnp.bfloat16)],
    )


def join_kernel(*refs, terms):
    total = refs[0][...].astype(jnp.float32)
    for ref in refs[1:terms]:
        total = total + ref[...].astype(jnp.float32)
    refs[-1][...] = total.astype(refs[-1].dtype)


def join(name, terms, after=()):
    return call(
        functools.partial(join_kernel, terms=len(terms)),
        name,
        like(*terms[0].shape),
        [VMEM] * (len(terms) + len(after)),
        (*terms, *after),
    )


def norm_kernel(place, gain_ref, hot_ref, *refs, parts, blocks):
    states, (sent_ref, own_ref, stat_ref) = refs[:-3], refs[-3:]
    chunk, width = states[0].shape
    gain = gain_ref[...].astype(jnp.float32)
    for m in range(parts):
        place_rows = slice(m * chunk, (m + 1) * chunk)
        rows = [states[k * parts + m][...].astype(jnp.float32) for k in range(blocks)]
        total = rows[0]
        for r in rows[1:]:
            total = total + r
        mean = jnp.sum(total, axis=-1, keepdims=True) / D
        rows = [r - mean for r in rows]
        total = rows[0] * rows[0]
        for r in rows[1:]:
            total = total + r * r
        variance = jnp.sum(total, axis=-1, keepdims=True) / D
        scale = lax.rsqrt(variance + 1e-05)
        own_ref[place_rows, :] = (rows[0] * scale * gain).astype(jnp.bfloat16)
        stat_ref[0, place_rows, :] = jnp.broadcast_to(mean, (chunk, HD))
        stat_ref[1, place_rows, :] = jnp.broadcast_to(scale, (chunk, HD))
    up_half(own_ref, hot_ref, place[2] ^ 1, sent_ref)


def up_half(rows_ref, hot_ref, half, out_ref):
    count = hot_ref.shape[0] // 2
    rows = rows_ref[...]
    for i in range(0, count, 2):
        at = half * count + i
        weight = jnp.concatenate([hot_ref[at], hot_ref[at + 1]], axis=1)
        out_ref[:, i * HD : (i + 2) * HD] = jnp.dot(
            rows, weight, preferred_element_type=jnp.float32
        ).astype(out_ref.dtype)


def norm(place, gain, hot, columns):
    blocks, parts = len(columns), len(columns[0])
    chunk, width = columns[0][0].shape
    rows = parts * chunk
    return call(
        functools.partial(norm_kernel, parts=parts, blocks=blocks),
        "norm_up_send",
        [
            like(rows, hot.shape[0] // 2 * HD),
            like(rows, width),
            jax.ShapeDtypeStruct((2, rows, HD), jnp.float32),
        ],
        [SMEM] + [VMEM] * (2 + blocks * parts),
        (place, gain, hot, *[a for column in columns for a in column]),
    )


def up_kernel(place, rows_ref, hot_ref, out_ref):
    up_half(rows_ref, hot_ref, place[2], out_ref)


def up_keep(place, rows, hot):
    return call(
        up_kernel,
        "up_keep",
        like(rows.shape[0], hot.shape[0] // 2 * HD),
        [SMEM, VMEM, VMEM],
        (place, rows, hot),
    )


def pieces_of(hidden, down_ref, block, width):
    depth = down_ref.shape[1]
    at = pl.ds(pl.multiple_of(block * width, width), width)
    weight = jnp.concatenate([down_ref[0, :, at], down_ref[1, :, at]], axis=0)
    return jnp.dot(hidden, weight, preferred_element_type=jnp.float32).astype(jnp.bfloat16)


def cold_kernel(place, counts, lists_ref, stat_ref, after, up_ref, down_ref, *refs, parts, steps):
    blocks = lists_ref.shape[0]
    gains, states = refs[:blocks], refs[blocks:-2]
    hidden_ref, out_ref = refs[-2:]
    chunk, width = states[0].shape
    total = parts * chunk
    here = chunk // steps
    b = place[1]
    mean, scale = stat_ref[0][:, :1], stat_ref[1][:, :1]
    sums = jnp.zeros((total, 2 * HD), jnp.float32)
    for k in range(blocks):
        rows = jnp.concatenate(
            [states[k * parts + m][...] for m in range(parts)], axis=0
        ).astype(jnp.float32)
        gain = gains[k][...].astype(jnp.float32)
        normed = ((rows - mean) * scale * gain).astype(jnp.bfloat16)
        at = pl.ds(pl.multiple_of((b ^ k) * width, width), width)
        weight = jnp.concatenate([up_ref[0, at, :], up_ref[1, at, :]], axis=1)
        sums = sums + jnp.dot(normed, weight, preferred_element_type=jnp.float32)
    slots = lists_ref.shape[3]
    index = lax.broadcasted_iota(jnp.int32, (total, slots), 0)
    slot = lax.broadcasted_iota(jnp.int32, (total, slots), 1)
    owner = (index // chunk) ^ place[0]
    row = (index // here % steps) * (parts * here) + owner * here + index % here
    halves = []
    for c in range(2):
        hit = (row == lists_ref[b, 0, c : c + 1, :]) & (slot < counts[2 * b + c])
        used = jnp.max(jnp.where(hit, 1.0, 0.0), axis=-1, keepdims=True)
        halves.append((jnp.maximum(sums[:, c * HD : (c + 1) * HD], 0.0) * used))
    hidden = jnp.concatenate(halves, axis=1).astype(jnp.bfloat16)
    hidden_ref[...] = hidden
    for i in range(blocks // 2):
        out_ref[i] = pieces_of(hidden, down_ref, b ^ (2 * i + 1), width)


def cold_send(place, counts, lists, stat, after, cold_up, cold_down, gains, columns, steps):
    blocks, parts = len(columns), len(columns[0])
    chunk, width = columns[0][0].shape
    rows = parts * chunk
    flat = [a for column in columns for a in column]
    return call(
        functools.partial(cold_kernel, parts=parts, steps=steps),
        "cold_send",
        [like(rows, 2 * HD), jax.ShapeDtypeStruct((blocks // 2, rows, width), jnp.bfloat16)],
        [SMEM, SMEM, VMEM, VMEM, AWAY, VMEM, VMEM] + [VMEM] * (blocks + len(flat)),
        (place, counts, lists, stat, after, cold_up, cold_down, *gains, *flat),
    )


def keep_kernel(place, hidden_ref, down_ref, after, near_ref, far_ref):
    width = near_ref.shape[1]
    hidden = hidden_ref[...]
    far_ref[...] = pieces_of(hidden, down_ref, place[1] ^ 2, width)
    near_ref[...] = pieces_of(hidden, down_ref, place[1], width)


def cold_keep(place, hidden, cold_down, after, width):
    rows = hidden.shape[0]
    return call(
        keep_kernel,
        "cold_keep",
        [like(rows, width), like(rows, width)],
        [SMEM, VMEM, VMEM, AWAY],
        (place, hidden, cold_down, after),
    )


def down_kernel(place, hidden_ref, hot_ref, *refs, half):
    count, depth = hot_ref.shape[0] // 2, hot_ref.shape[1]
    width = hot_ref.shape[2]
    wide = width // 3
    hidden = hidden_ref[...]
    first = (place[2] ^ half) * count
    for i in range(3):
        column = slice(i * wide, (i + 1) * wide)
        weight = hot_ref[pl.ds(first, count), :, column].reshape(count * depth, wide)
        made = jnp.dot(hidden, weight, preferred_element_type=jnp.float32)
        for ref in refs[:-1]:
            made = made + ref[:, column].astype(jnp.float32)
        refs[-1][:, column] = made


def down(place, half, hidden, hot, *before):
    return call(
        functools.partial(down_kernel, half=half),
        "down_got" if half else "down_keep",
        like(hidden.shape[0], hot.shape[2], jnp.float32),
        [SMEM, VMEM, VMEM] + [VMEM] * len(before),
        (place, hidden, hot, *before),
    )


def chunks_kernel(base_ref, more_ref, *outs):
    chunk = outs[0].shape[0]
    for m, out in enumerate(outs):
        rows = slice(m * chunk, (m + 1) * chunk)
        out[...] = (base_ref[rows, :] + more_ref[rows, :].astype(jnp.float32)).astype(out.dtype)


def into_chunks(base, more, parts):
    rows, width = base.shape
    return call(
        chunks_kernel,
        "into_chunks",
        [like(rows // parts, width, jnp.bfloat16 if m else jnp.float32) for m in range(parts)],
        [VMEM, VMEM],
        (base, more),
    )


def swap(x, axis, m, size=4):
    return lax.ppermute(x, axis, [(i, i ^ m) for i in range(size)])


def local_fast(
    queries,
    key_cache,
    value_cache,
    key_new,
    value_new,
    lengths,
    out_proj,
    residual,
    norm_gain,
    hot_up,
    hot_down,
    cold_up,
    cold_down,
    block_rows,
    block_counts,
):
    steps, here, _ = queries.shape
    all_rows, width = residual.shape[1:]
    parts = all_rows // here
    blocks = block_rows.shape[0]
    others = range(1, parts)
    b = lax.axis_index("blocks")
    h = lax.axis_index("heads")
    place = jnp.stack([h, b, b % 2]).astype(jnp.int32)
    counts = block_counts.reshape(-1)

    attended = attention(queries, key_cache, value_cache, key_new, value_new, lengths)
    across = swap(attended, "blocks", 2)
    gathered = [attended, swap(attended, "blocks", 1), across, swap(across, "blocks", 1)]
    pieces = project(place, gathered, out_proj)
    got = [swap(pieces[m], "heads", m) for m in others]
    (hot_up,) = load("load_up", pieces[1], hot_up)
    got, hot_up = lax.optimization_barrier((got, hot_up))
    gain = norm_gain[None]
    gains = [gain] + [swap(gain, "blocks", k) for k in range(1, blocks)]
    mine = lax.dynamic_slice(residual, (0, h * here, 0), (steps, here, width))
    state = join("join", [mine.reshape(steps * here, width), pieces[0], *got], gains[1:])
    states = [state] + [swap(state, "heads", m) for m in others]
    across = [swap(s, "blocks", 2) for s in states]
    columns = [
        states,
        [swap(s, "blocks", 1) for s in states],
        across,
        [swap(s, "blocks", 1) for s in across],
    ]
    sent, own, stat = norm(place, gain, hot_up, columns)
    sent = swap(sent, "blocks", 1)
    kept = up_keep(place, own, hot_up)
    summed = join("join_hot", [kept, sent])
    arrived = swap(summed, "blocks", 2)

    cold, cold_sent = cold_send(
        place, counts, block_rows, stat, summed, cold_up, cold_down, gains, columns, steps
    )
    cold_sent, arrived = lax.optimization_barrier((cold_sent, arrived))
    cold_got = swap(cold_sent, "blocks", 1)
    total = summed.astype(jnp.float32) + arrived.astype(jnp.float32)
    hidden = jnp.maximum(total, 0.0).astype(jnp.bfloat16)
    near, far = cold_keep(place, cold, cold_down, hidden, width)
    far = (far.astype(jnp.float32) + cold_got[1].astype(jnp.float32)).astype(jnp.bfloat16)
    partner = swap(hidden, "blocks", 1)
    hidden, far = lax.optimization_barrier((hidden, far))
    cold_far = swap(far, "blocks", 2)
    base = down(place, 0, hidden, hot_down)
    base = down(place, 1, partner, hot_down, base, near, cold_got[0])
    made = into_chunks(base, cold_far, parts)
    out = made[0]
    for m in others:
        out = out + swap(made[m], "heads", m).astype(jnp.float32)
    ffn_out = out.astype(jnp.bfloat16).reshape(steps, here, width)

    stacked = jnp.stack(states).reshape(parts, steps, 1, here, width)
    ordered = [
        lax.dynamic_index_in_dim(stacked, c ^ h, axis=0, keepdims=False) for c in range(parts)
    ]
    attn_state = jnp.concatenate(ordered, axis=1).reshape(steps, all_rows, width)
    return (attn_state, ffn_out)


def solution(mesh):
    placed = (
        P(None, ("groups", "blocks"), "heads"),
        P(("groups", "blocks"), None, "heads"),
        P(("groups", "blocks"), None, "heads"),
        P(None, ("groups", "blocks"), "heads"),
        P(None, ("groups", "blocks"), "heads"),
        P(("groups", "blocks")),
        P("heads", "blocks"),
        P(None, "groups", "blocks"),
        P("blocks"),
        P("heads", "blocks", None),
        P("heads", None, "blocks"),
        P(("blocks", "heads"), None, None),
        P(("blocks", "heads"), None, None),
        P("groups", "heads", None, None),
        P("groups", "heads", None),
    )
    sizes = tuple(mesh.shape[a] for a in ("blocks", "heads"))
    return jax.shard_map(
        local_fast if sizes == (4, 4) else local,
        mesh=mesh,
        in_specs=placed,
        out_specs=(P(None, "groups", "blocks"), P(None, ("groups", "heads"), "blocks")),
        check_vma=False,
    )
```

```python
import functools
import math

import jax
import jax.numpy as jnp
from jax import lax
from jax.experimental import pallas as pl
from jax.experimental.pallas import tpu as pltpu
from jax.sharding import PartitionSpec as P

HD = 128
D = 6144


def local(
    queries,
    key_cache,
    value_cache,
    key_new,
    value_new,
    lengths,
    out_proj,
    residual,
    norm_gain,
    hot_up,
    hot_down,
    cold_up,
    cold_down,
    block_rows,
    block_counts,
):
    steps, rows_here, width_here = queries.shape
    heads_here = width_here // HD
    context = key_cache.shape[1]
    query_heads = queries.reshape(steps, rows_here, heads_here, HD)
    cached_keys = key_cache.reshape(rows_here, context, heads_here, HD)
    cached_values = value_cache.reshape(rows_here, context, heads_here, HD)
    recent_keys = key_new.reshape(steps, rows_here, heads_here, HD)
    recent_values = value_new.reshape(steps, rows_here, heads_here, HD)
    factor = 1.0 / math.sqrt(HD)
    old_scores = (
        jnp.einsum("trhd,rphd->trhp", query_heads, cached_keys, preferred_element_type=jnp.float32)
        * factor
    )
    visible = jnp.arange(context)[None, :] < lengths[:, None]
    old_scores = jnp.where(visible[None, :, None, :], old_scores, -jnp.inf)
    new_scores = (
        jnp.einsum("trhd,srhd->trhs", query_heads, recent_keys, preferred_element_type=jnp.float32)
        * factor
    )
    causal = jnp.arange(steps)[None, :] <= jnp.arange(steps)[:, None]
    new_scores = jnp.where(causal[:, None, None, :], new_scores, -jnp.inf)
    highest = jnp.maximum(jnp.max(old_scores, axis=-1), jnp.max(new_scores, axis=-1))[..., None]
    old_weights = jnp.exp(old_scores - highest)
    new_weights = jnp.exp(new_scores - highest)
    denominator = jnp.sum(old_weights, axis=-1, keepdims=True) + jnp.sum(
        new_weights, axis=-1, keepdims=True
    )
    old_probs = (old_weights / denominator).astype(jnp.bfloat16)
    new_probs = (new_weights / denominator).astype(jnp.bfloat16)
    attended = jnp.einsum(
        "trhp,rphd->trhd", old_probs, cached_values, preferred_element_type=jnp.float32
    )
    attended = attended + jnp.einsum(
        "trhs,srhd->trhd", new_probs, recent_values, preferred_element_type=jnp.float32
    )
    attended = attended.reshape(steps, rows_here, width_here).astype(jnp.bfloat16)
    partial_out = jnp.einsum(
        "trk,kc->trc",
        lax.all_gather(attended, "blocks", axis=1, tiled=True),
        out_proj,
        preferred_element_type=jnp.float32,
    )
    summed = lax.psum(partial_out.astype(jnp.bfloat16), "heads").astype(jnp.float32)
    state = (residual.astype(jnp.float32) + summed).astype(jnp.bfloat16)
    state_wide = state.astype(jnp.float32)
    mean_row = lax.psum(jnp.sum(state_wide, axis=-1), "blocks") / D
    centred = state_wide - mean_row[..., None]
    variance = lax.psum(jnp.sum(centred * centred, axis=-1), "blocks") / D
    normed = (
        centred * lax.rsqrt(variance + 1e-05)[..., None] * norm_gain.astype(jnp.float32)
    ).astype(jnp.bfloat16)
    hot_inputs = jnp.einsum("trc,kch->trkh", normed, hot_up, preferred_element_type=jnp.float32)
    hot_total = lax.psum(hot_inputs.astype(jnp.bfloat16), "blocks").astype(jnp.float32)
    hot_hidden = jnp.maximum(hot_total, 0.0).astype(jnp.bfloat16)
    hot_sum = jnp.einsum("trkh,khc->trc", hot_hidden, hot_down, preferred_element_type=jnp.float32)
    all_rows = normed.shape[1]
    slice_width = normed.shape[2]
    flat_rows = normed.reshape(steps * all_rows, slice_width)
    slot_rows = block_rows[:, 0]
    slot_counts = block_counts[:, 0]
    outgoing = flat_rows[slot_rows]
    hidden = jnp.maximum(
        jnp.einsum(
            "ocnd,cdh->ocnh",
            lax.all_to_all(outgoing, "blocks", split_axis=0, concat_axis=3, tiled=True),
            cold_up,
            preferred_element_type=jnp.float32,
        ),
        0.0,
    ).astype(jnp.bfloat16)
    made = jnp.einsum(
        "ocnh,chd->ocnd", hidden, cold_down, preferred_element_type=jnp.float32
    ).astype(jnp.bfloat16)
    returned = lax.all_to_all(made, "blocks", split_axis=3, concat_axis=0, tiled=True)
    keep = jnp.arange(returned.shape[2])[None, None, :] < slot_counts[..., None]
    gained = jnp.where(keep[..., None], returned.astype(jnp.float32), 0.0)
    cold_sum = (
        jnp.zeros((steps * all_rows, slice_width), jnp.float32)
        .at[slot_rows.reshape(-1)]
        .add(gained.reshape(-1, slice_width))
    )
    total = cold_sum.reshape(steps, all_rows, slice_width) + hot_sum
    ffn_out = lax.psum_scatter(total.astype(jnp.bfloat16), "heads", scatter_dimension=1, tiled=True)
    return (state, ffn_out)


VMEM = pl.BlockSpec(memory_space=pltpu.VMEM)
SMEM = pl.BlockSpec(memory_space=pltpu.SMEM)
AWAY = pl.BlockSpec(memory_space=pl.ANY)
DMA = pltpu.SemaphoreType.DMA
COSTS = {"join": 60, "attention": 20, "norm_up_send": 20, "up_keep": 20, "cold_send": 30, "cold_keep": 0, "down": 0}
LIMITS = {"attention": 123, "load_project": 100, "load_up": 88, "load_cold": 72, "load_down": 84}


def call(kernel, name, out_shape, specs, operands, scratch=()):
    return pl.pallas_call(
        kernel,
        in_specs=specs,
        out_specs=jax.tree.map(lambda _: VMEM, out_shape),
        out_shape=out_shape,
        scratch_shapes=list(scratch),
        compiler_params=pltpu.CompilerParams(vmem_limit_bytes=LIMITS.get(name, 24) * 2**19),
        cost_estimate=pl.CostEstimate(
            flops=0, bytes_accessed=COSTS.get(name, 10) * 10**6, transcendentals=0
        ),
        name=name,
    )(*operands)


def begin(copies):
    for copy in copies:
        copy.start()


def finish(copies):
    for copy in copies:
        copy.wait()


def like(rows, width, dtype=jnp.bfloat16):
    return jax.ShapeDtypeStruct((rows, width), dtype)


def load_kernel(after, *refs):
    count = (len(refs) - 1) // 2
    copies = [
        pltpu.make_async_copy(source, target, refs[-1].at[i])
        for i, (source, target) in enumerate(zip(refs[:count], refs[count:-1]))
    ]
    begin(copies)
    finish(copies)


def load(name, after, *arrays):
    return call(
        load_kernel,
        name,
        [jax.ShapeDtypeStruct(a.shape, a.dtype) for a in arrays],
        [AWAY] * (1 + len(arrays)),
        (after, *arrays),
        [DMA((len(arrays),))],
    )


def attention_kernel(
    lengths, q, kn, vn, keys, values, out_ref, small, key_buf, value_buf, own_buf, prob_buf, sum_buf,
    small_sems, sems, *, here, steps,
):
    rows, width = q.shape
    context = keys.shape[0] // here
    wide = 2 * HD
    parts = wide // HD
    count = width // wide
    step_rows = 8
    deep = step_rows * context
    turns = here // step_rows
    heads = [
        pltpu.make_async_copy(ref, small.at[i], small_sems.at[i]) for i, ref in enumerate((q, kn, vn))
    ]
    key_copies, value_copies = (
        [
            pltpu.make_async_copy(
                ref.at[pl.ds(j * deep, deep)], buf.at[pl.ds(j * deep, deep)], sems.at[which, j]
            )
            for j in range(turns)
        ]
        for which, (ref, buf) in enumerate(((keys, key_buf), (values, value_buf)))
    )
    begin(heads + key_copies + value_copies)

    nt = (((1,), (1,)), ((), ()))
    factor = 1.0 / math.sqrt(HD)
    lane_head = lax.broadcasted_iota(jnp.int32, (rows, wide), 1) // HD
    row = lax.broadcasted_iota(jnp.int32, (parts * rows, context), 0) % here
    slot = lax.broadcasted_iota(jnp.int32, (parts * rows, context), 1)
    limit = jnp.zeros_like(slot)
    for r in range(here):
        limit = jnp.where(row == r, lengths[r], limit)
    open_slot = slot < limit
    at = lax.broadcasted_iota(jnp.int32, (parts * rows, rows), 0) % rows
    to = lax.broadcasted_iota(jnp.int32, (parts * rows, rows), 1)
    seen = (at % here == to % here) & (to // here <= at // here)
    columns = [slice(i * wide, (i + 1) * wide) for i in range(count)]
    finish(heads)
    splits = []
    for column in columns:
        mine = small[0, :, column]
        splits.append(
            jnp.concatenate(
                [jnp.where(lane_head == j, mine, jnp.zeros_like(mine)) for j in range(parts)], axis=0
            )
        )
    for j in range(turns):
        key_copies[j].wait()
        for i, column in enumerate(columns):
            scores = lax.dot_general(
                splits[i],
                key_buf[j * deep : (j + 1) * deep, column],
                nt,
                preferred_element_type=jnp.float32,
            )
            own = own_buf[i] if j else scores[:, :context]
            for r in range(step_rows):
                own = jnp.where(
                    row == j * step_rows + r, scores[:, r * context : (r + 1) * context], own
                )
            own_buf[i] = own
    for i, column in enumerate(columns):
        fresh = lax.dot_general(
            splits[i], small[1, :, column], nt, preferred_element_type=jnp.float32
        )
        fresh = jnp.where(seen, fresh * factor, -jnp.inf)
        own = jnp.where(open_slot, own_buf[i] * factor, -jnp.inf)
        top = jnp.maximum(
            jnp.max(own, axis=-1, keepdims=True), jnp.max(fresh, axis=-1, keepdims=True)
        )
        own = jnp.exp(own - top)
        fresh = jnp.exp(fresh - top)
        scale = 1.0 / (
            jnp.sum(own, axis=-1, keepdims=True) + jnp.sum(fresh, axis=-1, keepdims=True)
        )
        prob_buf[i] = own * scale
        sum_buf[i] = jnp.dot(
            (fresh * scale).astype(jnp.bfloat16),
            small[2, :, column],
            preferred_element_type=jnp.float32,
        )
    for j in range(turns):
        value_copies[j].wait()
        for i, column in enumerate(columns):
            probs = prob_buf[i]
            spread = jnp.concatenate(
                [
                    jnp.where(row == j * step_rows + r, probs, 0.0).astype(jnp.bfloat16)
                    for r in range(step_rows)
                ],
                axis=1,
            )
            got = sum_buf[i] + jnp.dot(
                spread,
                value_buf[j * deep : (j + 1) * deep, column],
                preferred_element_type=jnp.float32,
            )
            if j + 1 < turns:
                sum_buf[i] = got
            else:
                answer = got[:rows]
                for p in range(1, parts):
                    answer = jnp.where(lane_head == p, got[p * rows : (p + 1) * rows], answer)
                out_ref[:, column] = answer.astype(jnp.bfloat16)


def attention(queries, key_cache, value_cache, key_new, value_new, lengths):
    steps, here, width = queries.shape
    context = key_cache.shape[1]
    rows = steps * here
    count = width // (2 * HD)
    flat = lambda a: a.reshape(-1, width)
    return call(
        functools.partial(attention_kernel, here=here, steps=steps),
        "attention",
        like(rows, width),
        [SMEM] + [AWAY] * 5,
        (
            lengths,
            flat(queries),
            flat(key_new),
            flat(value_new),
            flat(key_cache),
            flat(value_cache),
        ),
        [
            pltpu.VMEM((3, rows, width), jnp.bfloat16),
            pltpu.VMEM((here * context, width), jnp.bfloat16),
            pltpu.VMEM((here * context, width), jnp.bfloat16),
            pltpu.VMEM((count, 2 * rows, context), jnp.float32),
            pltpu.VMEM((count, 2 * rows, context), jnp.float32),
            pltpu.VMEM((count, 2 * rows, 2 * HD), jnp.float32),
            DMA((3,)),
            DMA((2, here // 8)),
        ],
    )


def project_kernel(place, *refs, parts):
    rows_refs, weight_ref, outs, held = refs[:parts], refs[parts], refs[parts + 1 : -1], refs[-1]
    chunk = outs[0].shape[0]
    for k, ref in enumerate(rows_refs):
        held[k] = ref[...]
    rows = jnp.concatenate([held[place[0] ^ place[1] ^ m] for m in range(parts)], axis=0)
    width = weight_ref.shape[1]
    wide = width // 3
    for i in range(3):
        column = slice(i * wide, (i + 1) * wide)
        made = jnp.dot(rows, weight_ref[:, column], preferred_element_type=jnp.float32)
        for m, out in enumerate(outs):
            out[:, column] = made[m * chunk : (m + 1) * chunk].astype(out.dtype)


def project(place, gathered, weight):
    parts = len(gathered)
    chunk, depth = gathered[0].shape
    width = weight.shape[1]
    return call(
        functools.partial(project_kernel, parts=parts),
        "project",
        [like(chunk, width, jnp.bfloat16 if m else jnp.float32) for m in range(parts)],
        [SMEM] + [VMEM] * (parts + 1),
        (place, *gathered, weight),
        [pltpu.VMEM((parts, chunk, depth), jnp.bfloat16)],
    )


def join_kernel(*refs, terms):
    total = refs[0][...].astype(jnp.float32)
    for ref in refs[1:terms]:
        total = total + ref[...].astype(jnp.float32)
    refs[-1][...] = total.astype(refs[-1].dtype)


def join(name, terms, after=()):
    return call(
        functools.partial(join_kernel, terms=len(terms)),
        name,
        like(*terms[0].shape),
        [VMEM] * (len(terms) + len(after)),
        (*terms, *after),
    )


def norm_kernel(place, gain_ref, hot_ref, *refs, parts, blocks):
    states, (sent_ref, own_ref, stat_ref) = refs[:-3], refs[-3:]
    chunk, width = states[0].shape
    gain = gain_ref[...].astype(jnp.float32)
    for m in range(parts):
        place_rows = slice(m * chunk, (m + 1) * chunk)
        rows = [states[k * parts + m][...].astype(jnp.float32) for k in range(blocks)]
        total = rows[0]
        for r in rows[1:]:
            total = total + r
        mean = jnp.sum(total, axis=-1, keepdims=True) / D
        rows = [r - mean for r in rows]
        total = rows[0] * rows[0]
        for r in rows[1:]:
            total = total + r * r
        variance = jnp.sum(total, axis=-1, keepdims=True) / D
        scale = lax.rsqrt(variance + 1e-05)
        own_ref[place_rows, :] = (rows[0] * scale * gain).astype(jnp.bfloat16)
        stat_ref[0, place_rows, :] = jnp.broadcast_to(mean, (chunk, HD))
        stat_ref[1, place_rows, :] = jnp.broadcast_to(scale, (chunk, HD))
    up_half(own_ref, hot_ref, place[2] ^ 1, sent_ref)


def up_half(rows_ref, hot_ref, half, out_ref):
    count = hot_ref.shape[0] // 2
    rows = rows_ref[...]
    for i in range(0, count, 2):
        at = half * count + i
        weight = jnp.concatenate([hot_ref[at], hot_ref[at + 1]], axis=1)
        out_ref[:, i * HD : (i + 2) * HD] = jnp.dot(
            rows, weight, preferred_element_type=jnp.float32
        ).astype(out_ref.dtype)


def norm(place, gain, hot, columns):
    blocks, parts = len(columns), len(columns[0])
    chunk, width = columns[0][0].shape
    rows = parts * chunk
    return call(
        functools.partial(norm_kernel, parts=parts, blocks=blocks),
        "norm_up_send",
        [
            like(rows, hot.shape[0] // 2 * HD),
            like(rows, width),
            jax.ShapeDtypeStruct((2, rows, HD), jnp.float32),
        ],
        [SMEM] + [VMEM] * (2 + blocks * parts),
        (place, gain, hot, *[a for column in columns for a in column]),
    )


def up_kernel(place, rows_ref, hot_ref, out_ref):
    up_half(rows_ref, hot_ref, place[2], out_ref)


def up_keep(place, rows, hot):
    return call(
        up_kernel,
        "up_keep",
        like(rows.shape[0], hot.shape[0] // 2 * HD),
        [SMEM, VMEM, VMEM],
        (place, rows, hot),
    )


def pieces_of(hidden, down_ref, block, width):
    depth = down_ref.shape[1]
    at = pl.ds(pl.multiple_of(block * width, width), width)
    weight = jnp.concatenate([down_ref[0, :, at], down_ref[1, :, at]], axis=0)
    return jnp.dot(hidden, weight, preferred_element_type=jnp.float32).astype(jnp.bfloat16)


def cold_kernel(place, counts, lists_ref, stat_ref, after, up_ref, down_ref, *refs, parts, steps):
    blocks = lists_ref.shape[0]
    gains, states = refs[:blocks], refs[blocks:-3]
    near_ref, out_ref, far_ref = refs[-3:]
    chunk, width = states[0].shape
    total = parts * chunk
    here = chunk // steps
    b = place[1]
    mean, scale = stat_ref[0][:, :1], stat_ref[1][:, :1]
    sums = jnp.zeros((total, 2 * HD), jnp.float32)
    for k in range(blocks):
        rows = jnp.concatenate(
            [states[k * parts + m][...] for m in range(parts)], axis=0
        ).astype(jnp.float32)
        gain = gains[k][...].astype(jnp.float32)
        normed = ((rows - mean) * scale * gain).astype(jnp.bfloat16)
        at = pl.ds(pl.multiple_of((b ^ k) * width, width), width)
        weight = jnp.concatenate([up_ref[0, at, :], up_ref[1, at, :]], axis=1)
        sums = sums + jnp.dot(normed, weight, preferred_element_type=jnp.float32)
    slots = lists_ref.shape[3]
    index = lax.broadcasted_iota(jnp.int32, (total, slots), 0)
    slot = lax.broadcasted_iota(jnp.int32, (total, slots), 1)
    owner = (index // chunk) ^ place[0]
    row = (index // here % steps) * (parts * here) + owner * here + index % here
    halves = []
    for c in range(2):
        hit = (row == lists_ref[b, 0, c : c + 1, :]) & (slot < counts[2 * b + c])
        used = jnp.max(jnp.where(hit, 1.0, 0.0), axis=-1, keepdims=True)
        halves.append((jnp.maximum(sums[:, c * HD : (c + 1) * HD], 0.0) * used))
    hidden = jnp.concatenate(halves, axis=1).astype(jnp.bfloat16)
    for i in range(blocks // 2):
        out_ref[i] = pieces_of(hidden, down_ref, b ^ (2 * i + 1), width)
    far_ref[...] = pieces_of(hidden, down_ref, b ^ 2, width)
    near_ref[...] = pieces_of(hidden, down_ref, b, width)


def cold_send(place, counts, lists, stat, after, cold_up, cold_down, gains, columns, steps):
    blocks, parts = len(columns), len(columns[0])
    chunk, width = columns[0][0].shape
    rows = parts * chunk
    flat = [a for column in columns for a in column]
    return call(
        functools.partial(cold_kernel, parts=parts, steps=steps),
        "cold_send",
        [
            like(rows, width),
            jax.ShapeDtypeStruct((blocks // 2, rows, width), jnp.bfloat16),
            like(rows, width),
        ],
        [SMEM, SMEM, VMEM, VMEM, AWAY, VMEM, VMEM] + [VMEM] * (blocks + len(flat)),
        (place, counts, lists, stat, after, cold_up, cold_down, *gains, *flat),
    )


def down_kernel(place, hidden_ref, partner_ref, hot_ref, *refs):
    count, depth = hot_ref.shape[0] // 2, hot_ref.shape[1]
    width = hot_ref.shape[2]
    wide = width // 3
    for i in range(3):
        column = slice(i * wide, (i + 1) * wide)
        made = refs[0][:, column].astype(jnp.float32)
        for ref in refs[1:-1]:
            made = made + ref[:, column].astype(jnp.float32)
        for half, rows_ref in enumerate((hidden_ref, partner_ref)):
            first = (place[2] ^ half) * count
            weight = hot_ref[pl.ds(first, count), :, column].reshape(count * depth, wide)
            made = made + jnp.dot(rows_ref[...], weight, preferred_element_type=jnp.float32)
        refs[-1][:, column] = made


def down(place, hidden, partner, hot, *before):
    return call(
        down_kernel,
        "down",
        like(hidden.shape[0], hot.shape[2], jnp.float32),
        [SMEM] + [VMEM] * (3 + len(before)),
        (place, hidden, partner, hot, *before),
    )


def chunks_kernel(base_ref, more_ref, *outs, first):
    chunk = outs[0].shape[0]
    for i, out in enumerate(outs):
        rows = slice(i * chunk, (i + 1) * chunk)
        from_base = slice((first + i) * chunk, (first + i + 1) * chunk)
        out[...] = (base_ref[from_base, :] + more_ref[rows, :].astype(jnp.float32)).astype(out.dtype)


def into_chunks(base, more, first, parts):
    width = base.shape[1]
    count = parts // 2
    chunk = more.shape[0] // count
    return call(
        functools.partial(chunks_kernel, first=first),
        "chunks_early" if first else "chunks_late",
        [like(chunk, width, jnp.bfloat16 if first + i else jnp.float32) for i in range(count)],
        [VMEM, VMEM],
        (base, more),
    )


def swap(x, axis, m, size=4):
    return lax.ppermute(x, axis, [(i, i ^ m) for i in range(size)])


def local_fast(
    queries,
    key_cache,
    value_cache,
    key_new,
    value_new,
    lengths,
    out_proj,
    residual,
    norm_gain,
    hot_up,
    hot_down,
    cold_up,
    cold_down,
    block_rows,
    block_counts,
):
    steps, here, _ = queries.shape
    all_rows, width = residual.shape[1:]
    parts = all_rows // here
    blocks = block_rows.shape[0]
    others = range(parts - 1, 0, -1)
    b = lax.axis_index("blocks")
    h = lax.axis_index("heads")
    place = jnp.stack([h, b, b % 2]).astype(jnp.int32)
    counts = block_counts.reshape(-1)

    attended = attention(queries, key_cache, value_cache, key_new, value_new, lengths)
    across = swap(attended, "blocks", 2)
    gathered = [attended, swap(attended, "blocks", 1), across, swap(across, "blocks", 1)]
    gain = norm_gain[None]
    gains = [gain] + [swap(gain, "blocks", k) for k in range(1, blocks)]
    gathered, gains = lax.optimization_barrier((gathered, gains))
    pieces = project(place, gathered, out_proj)
    got = [swap(pieces[m], "heads", m) for m in others]
    (hot_up,) = load("load_up", pieces[1], hot_up)
    got, hot_up = lax.optimization_barrier((got, hot_up))
    mine = lax.dynamic_slice(residual, (0, h * here, 0), (steps, here, width))
    state = join("join", [mine.reshape(steps * here, width), pieces[0], *got])
    moved = {m: swap(state, "heads", m) for m in others}
    states = [state] + [moved[m] for m in range(1, parts)]
    across = [swap(s, "blocks", 2) for s in states]
    columns = [
        states,
        [swap(s, "blocks", 1) for s in states],
        across,
        [swap(s, "blocks", 1) for s in across],
    ]
    sent, own, stat = norm(place, gain, hot_up, columns)
    sent = swap(sent, "blocks", 1)
    kept = up_keep(place, own, hot_up)
    summed = join("join_hot", [kept, sent])
    arrived = swap(summed, "blocks", 2)

    near, cold_sent, far = cold_send(
        place, counts, block_rows, stat, summed, cold_up, cold_down, gains, columns, steps
    )
    cold_sent, arrived = lax.optimization_barrier((cold_sent, arrived))
    cold_got = swap(cold_sent, "blocks", 1)
    total = summed.astype(jnp.float32) + arrived.astype(jnp.float32)
    hidden = jnp.maximum(total, 0.0).astype(jnp.bfloat16)
    far = far.astype(jnp.float32) + cold_got[1].astype(jnp.float32)
    half = far.shape[0] // 2
    late, early = far[:half].astype(jnp.bfloat16), far[half:].astype(jnp.bfloat16)
    partner = swap(hidden, "blocks", 1)
    hidden, late, early = lax.optimization_barrier((hidden, late, early))
    early = swap(early, "blocks", 2)
    late = swap(late, "blocks", 2)
    base = down(place, hidden, partner, hot_down, near, cold_got[0])
    made = into_chunks(base, early, parts // 2, parts)
    arrived = [
        swap(made[i], "heads", parts // 2 + i) for i in reversed(range(parts // 2))
    ]
    made, late = lax.optimization_barrier((made, late))
    made = into_chunks(base, late, 0, parts)
    arrived += [swap(made[i], "heads", i) for i in range(1, parts // 2)]
    out = made[0]
    for piece in arrived:
        out = out + piece.astype(jnp.float32)
    ffn_out = out.astype(jnp.bfloat16).reshape(steps, here, width)

    stacked = jnp.stack(states).reshape(parts, steps, 1, here, width)
    ordered = [
        lax.dynamic_index_in_dim(stacked, c ^ h, axis=0, keepdims=False) for c in range(parts)
    ]
    attn_state = jnp.concatenate(ordered, axis=1).reshape(steps, all_rows, width)
    return (attn_state, ffn_out)


def solution(mesh):
    placed = (
        P(None, ("groups", "blocks"), "heads"),
        P(("groups", "blocks"), None, "heads"),
        P(("groups", "blocks"), None, "heads"),
        P(None, ("groups", "blocks"), "heads"),
        P(None, ("groups", "blocks"), "heads"),
        P(("groups", "blocks")),
        P("heads", "blocks"),
        P(None, "groups", "blocks"),
        P("blocks"),
        P("heads", "blocks", None),
        P("heads", None, "blocks"),
        P(("blocks", "heads"), None, None),
        P(("blocks", "heads"), None, None),
        P("groups", "heads", None, None),
        P("groups", "heads", None),
    )
    sizes = tuple(mesh.shape[a] for a in ("blocks", "heads"))
    return jax.shard_map(
        local_fast if sizes == (4, 4) else local,
        mesh=mesh,
        in_specs=placed,
        out_specs=(P(None, "groups", "blocks"), P(None, ("groups", "heads"), "blocks")),
        check_vma=False,
    )
```

```python
import functools
import math

import jax
import jax.numpy as jnp
from jax import lax
from jax.experimental import pallas as pl
from jax.experimental.pallas import tpu as pltpu
from jax.sharding import PartitionSpec as P

HD = 128
D = 6144


def local(
    queries,
    key_cache,
    value_cache,
    key_new,
    value_new,
    lengths,
    out_proj,
    residual,
    norm_gain,
    hot_up,
    hot_down,
    cold_up,
    cold_down,
    block_rows,
    block_counts,
):
    steps, rows_here, width_here = queries.shape
    heads_here = width_here // HD
    context = key_cache.shape[1]
    query_heads = queries.reshape(steps, rows_here, heads_here, HD)
    cached_keys = key_cache.reshape(rows_here, context, heads_here, HD)
    cached_values = value_cache.reshape(rows_here, context, heads_here, HD)
    recent_keys = key_new.reshape(steps, rows_here, heads_here, HD)
    recent_values = value_new.reshape(steps, rows_here, heads_here, HD)
    factor = 1.0 / math.sqrt(HD)
    old_scores = (
        jnp.einsum("trhd,rphd->trhp", query_heads, cached_keys, preferred_element_type=jnp.float32)
        * factor
    )
    visible = jnp.arange(context)[None, :] < lengths[:, None]
    old_scores = jnp.where(visible[None, :, None, :], old_scores, -jnp.inf)
    new_scores = (
        jnp.einsum("trhd,srhd->trhs", query_heads, recent_keys, preferred_element_type=jnp.float32)
        * factor
    )
    causal = jnp.arange(steps)[None, :] <= jnp.arange(steps)[:, None]
    new_scores = jnp.where(causal[:, None, None, :], new_scores, -jnp.inf)
    highest = jnp.maximum(jnp.max(old_scores, axis=-1), jnp.max(new_scores, axis=-1))[..., None]
    old_weights = jnp.exp(old_scores - highest)
    new_weights = jnp.exp(new_scores - highest)
    denominator = jnp.sum(old_weights, axis=-1, keepdims=True) + jnp.sum(
        new_weights, axis=-1, keepdims=True
    )
    old_probs = (old_weights / denominator).astype(jnp.bfloat16)
    new_probs = (new_weights / denominator).astype(jnp.bfloat16)
    attended = jnp.einsum(
        "trhp,rphd->trhd", old_probs, cached_values, preferred_element_type=jnp.float32
    )
    attended = attended + jnp.einsum(
        "trhs,srhd->trhd", new_probs, recent_values, preferred_element_type=jnp.float32
    )
    attended = attended.reshape(steps, rows_here, width_here).astype(jnp.bfloat16)
    partial_out = jnp.einsum(
        "trk,kc->trc",
        lax.all_gather(attended, "blocks", axis=1, tiled=True),
        out_proj,
        preferred_element_type=jnp.float32,
    )
    summed = lax.psum(partial_out.astype(jnp.bfloat16), "heads").astype(jnp.float32)
    state = (residual.astype(jnp.float32) + summed).astype(jnp.bfloat16)
    state_wide = state.astype(jnp.float32)
    mean_row = lax.psum(jnp.sum(state_wide, axis=-1), "blocks") / D
    centred = state_wide - mean_row[..., None]
    variance = lax.psum(jnp.sum(centred * centred, axis=-1), "blocks") / D
    normed = (
        centred * lax.rsqrt(variance + 1e-05)[..., None] * norm_gain.astype(jnp.float32)
    ).astype(jnp.bfloat16)
    hot_inputs = jnp.einsum("trc,kch->trkh", normed, hot_up, preferred_element_type=jnp.float32)
    hot_total = lax.psum(hot_inputs.astype(jnp.bfloat16), "blocks").astype(jnp.float32)
    hot_hidden = jnp.maximum(hot_total, 0.0).astype(jnp.bfloat16)
    hot_sum = jnp.einsum("trkh,khc->trc", hot_hidden, hot_down, preferred_element_type=jnp.float32)
    all_rows = normed.shape[1]
    slice_width = normed.shape[2]
    flat_rows = normed.reshape(steps * all_rows, slice_width)
    slot_rows = block_rows[:, 0]
    slot_counts = block_counts[:, 0]
    outgoing = flat_rows[slot_rows]
    hidden = jnp.maximum(
        jnp.einsum(
            "ocnd,cdh->ocnh",
            lax.all_to_all(outgoing, "blocks", split_axis=0, concat_axis=3, tiled=True),
            cold_up,
            preferred_element_type=jnp.float32,
        ),
        0.0,
    ).astype(jnp.bfloat16)
    made = jnp.einsum(
        "ocnh,chd->ocnd", hidden, cold_down, preferred_element_type=jnp.float32
    ).astype(jnp.bfloat16)
    returned = lax.all_to_all(made, "blocks", split_axis=3, concat_axis=0, tiled=True)
    keep = jnp.arange(returned.shape[2])[None, None, :] < slot_counts[..., None]
    gained = jnp.where(keep[..., None], returned.astype(jnp.float32), 0.0)
    cold_sum = (
        jnp.zeros((steps * all_rows, slice_width), jnp.float32)
        .at[slot_rows.reshape(-1)]
        .add(gained.reshape(-1, slice_width))
    )
    total = cold_sum.reshape(steps, all_rows, slice_width) + hot_sum
    ffn_out = lax.psum_scatter(total.astype(jnp.bfloat16), "heads", scatter_dimension=1, tiled=True)
    return (state, ffn_out)


VMEM = pl.BlockSpec(memory_space=pltpu.VMEM)
SMEM = pl.BlockSpec(memory_space=pltpu.SMEM)
AWAY = pl.BlockSpec(memory_space=pl.ANY)
DMA = pltpu.SemaphoreType.DMA
COSTS = {"hold": 60, "join": 60, "attention": 20, "norm_up_send": 20, "up_keep": 20, "cold_send": 30, "cold_keep": 0, "down": 0}
LIMITS = {"attention": 123, "load_project": 100, "load_up": 88, "load_cold": 72, "load_down": 84}


def call(kernel, name, out_shape, specs, operands, scratch=()):
    return pl.pallas_call(
        kernel,
        in_specs=specs,
        out_specs=jax.tree.map(lambda _: VMEM, out_shape),
        out_shape=out_shape,
        scratch_shapes=list(scratch),
        compiler_params=pltpu.CompilerParams(vmem_limit_bytes=LIMITS.get(name, 24) * 2**19),
        cost_estimate=pl.CostEstimate(
            flops=0, bytes_accessed=COSTS.get(name, 10) * 10**6, transcendentals=0
        ),
        name=name,
    )(*operands)


def begin(copies):
    for copy in copies:
        copy.start()


def finish(copies):
    for copy in copies:
        copy.wait()


def like(rows, width, dtype=jnp.bfloat16):
    return jax.ShapeDtypeStruct((rows, width), dtype)


def load_kernel(after, *refs):
    count = (len(refs) - 1) // 2
    copies = [
        pltpu.make_async_copy(source, target, refs[-1].at[i])
        for i, (source, target) in enumerate(zip(refs[:count], refs[count:-1]))
    ]
    begin(copies)
    finish(copies)


def load(name, after, *arrays):
    return call(
        load_kernel,
        name,
        [jax.ShapeDtypeStruct(a.shape, a.dtype) for a in arrays],
        [AWAY] * (1 + len(arrays)),
        (after, *arrays),
        [DMA((len(arrays),))],
    )


def attention_kernel(
    lengths, q, kn, vn, keys, values, out_ref, small, key_buf, value_buf, own_buf, prob_buf, sum_buf,
    small_sems, sems, *, here, steps,
):
    rows, width = q.shape
    context = keys.shape[0] // here
    wide = 2 * HD
    parts = wide // HD
    count = width // wide
    step_rows = 8
    deep = step_rows * context
    turns = here // step_rows
    heads = [
        pltpu.make_async_copy(ref, small.at[i], small_sems.at[i]) for i, ref in enumerate((q, kn, vn))
    ]
    key_copies, value_copies = (
        [
            pltpu.make_async_copy(
                ref.at[pl.ds(j * deep, deep)], buf.at[pl.ds(j * deep, deep)], sems.at[which, j]
            )
            for j in range(turns)
        ]
        for which, (ref, buf) in enumerate(((keys, key_buf), (values, value_buf)))
    )
    begin(heads + key_copies + value_copies)

    nt = (((1,), (1,)), ((), ()))
    factor = 1.0 / math.sqrt(HD)
    lane_head = lax.broadcasted_iota(jnp.int32, (rows, wide), 1) // HD
    row = lax.broadcasted_iota(jnp.int32, (parts * rows, context), 0) % here
    slot = lax.broadcasted_iota(jnp.int32, (parts * rows, context), 1)
    limit = jnp.zeros_like(slot)
    for r in range(here):
        limit = jnp.where(row == r, lengths[r], limit)
    open_slot = slot < limit
    at = lax.broadcasted_iota(jnp.int32, (parts * rows, rows), 0) % rows
    to = lax.broadcasted_iota(jnp.int32, (parts * rows, rows), 1)
    seen = (at % here == to % here) & (to // here <= at // here)
    columns = [slice(i * wide, (i + 1) * wide) for i in range(count)]
    finish(heads)
    splits = []
    for column in columns:
        mine = small[0, :, column]
        splits.append(
            jnp.concatenate(
                [jnp.where(lane_head == j, mine, jnp.zeros_like(mine)) for j in range(parts)], axis=0
            )
        )
    for j in range(turns):
        key_copies[j].wait()
        for i, column in enumerate(columns):
            scores = lax.dot_general(
                splits[i],
                key_buf[j * deep : (j + 1) * deep, column],
                nt,
                preferred_element_type=jnp.float32,
            )
            own = own_buf[i] if j else scores[:, :context]
            for r in range(step_rows):
                own = jnp.where(
                    row == j * step_rows + r, scores[:, r * context : (r + 1) * context], own
                )
            own_buf[i] = own
    for i, column in enumerate(columns):
        fresh = lax.dot_general(
            splits[i], small[1, :, column], nt, preferred_element_type=jnp.float32
        )
        fresh = jnp.where(seen, fresh * factor, -jnp.inf)
        own = jnp.where(open_slot, own_buf[i] * factor, -jnp.inf)
        top = jnp.maximum(
            jnp.max(own, axis=-1, keepdims=True), jnp.max(fresh, axis=-1, keepdims=True)
        )
        own = jnp.exp(own - top)
        fresh = jnp.exp(fresh - top)
        scale = 1.0 / (
            jnp.sum(own, axis=-1, keepdims=True) + jnp.sum(fresh, axis=-1, keepdims=True)
        )
        prob_buf[i] = own * scale
        sum_buf[i] = jnp.dot(
            (fresh * scale).astype(jnp.bfloat16),
            small[2, :, column],
            preferred_element_type=jnp.float32,
        )
    for j in range(turns):
        value_copies[j].wait()
        for i, column in enumerate(columns):
            probs = prob_buf[i]
            spread = jnp.concatenate(
                [
                    jnp.where(row == j * step_rows + r, probs, 0.0).astype(jnp.bfloat16)
                    for r in range(step_rows)
                ],
                axis=1,
            )
            got = sum_buf[i] + jnp.dot(
                spread,
                value_buf[j * deep : (j + 1) * deep, column],
                preferred_element_type=jnp.float32,
            )
            if j + 1 < turns:
                sum_buf[i] = got
            else:
                answer = got[:rows]
                for p in range(1, parts):
                    answer = jnp.where(lane_head == p, got[p * rows : (p + 1) * rows], answer)
                out_ref[:, column] = answer.astype(jnp.bfloat16)


def attention(queries, key_cache, value_cache, key_new, value_new, lengths):
    steps, here, width = queries.shape
    context = key_cache.shape[1]
    rows = steps * here
    count = width // (2 * HD)
    flat = lambda a: a.reshape(-1, width)
    return call(
        functools.partial(attention_kernel, here=here, steps=steps),
        "attention",
        like(rows, width),
        [SMEM] + [AWAY] * 5,
        (
            lengths,
            flat(queries),
            flat(key_new),
            flat(value_new),
            flat(key_cache),
            flat(value_cache),
        ),
        [
            pltpu.VMEM((3, rows, width), jnp.bfloat16),
            pltpu.VMEM((here * context, width), jnp.bfloat16),
            pltpu.VMEM((here * context, width), jnp.bfloat16),
            pltpu.VMEM((count, 2 * rows, context), jnp.float32),
            pltpu.VMEM((count, 2 * rows, context), jnp.float32),
            pltpu.VMEM((count, 2 * rows, 2 * HD), jnp.float32),
            DMA((3,)),
            DMA((2, here // 8)),
        ],
    )


def project_kernel(place, *refs, parts):
    rows_refs, weight_ref, outs, held = refs[:parts], refs[parts], refs[parts + 1 : -1], refs[-1]
    chunk = outs[0].shape[0]
    for k, ref in enumerate(rows_refs):
        held[k] = ref[...]
    rows = jnp.concatenate([held[place[0] ^ place[1] ^ m] for m in range(parts)], axis=0)
    width = weight_ref.shape[1]
    wide = width // 3
    for i in range(3):
        column = slice(i * wide, (i + 1) * wide)
        made = jnp.dot(rows, weight_ref[:, column], preferred_element_type=jnp.float32)
        for m, out in enumerate(outs):
            out[:, column] = made[m * chunk : (m + 1) * chunk].astype(out.dtype)


def project(place, gathered, weight):
    parts = len(gathered)
    chunk, depth = gathered[0].shape
    width = weight.shape[1]
    return call(
        functools.partial(project_kernel, parts=parts),
        "project",
        [like(chunk, width, jnp.bfloat16 if m else jnp.float32) for m in range(parts)],
        [SMEM] + [VMEM] * (parts + 1),
        (place, *gathered, weight),
        [pltpu.VMEM((parts, chunk, depth), jnp.bfloat16)],
    )


def join_kernel(*refs, terms):
    total = refs[0][...].astype(jnp.float32)
    for ref in refs[1:terms]:
        total = total + ref[...].astype(jnp.float32)
    refs[-1][...] = total.astype(refs[-1].dtype)


def join(name, terms, after=()):
    return call(
        functools.partial(join_kernel, terms=len(terms)),
        name,
        like(*terms[0].shape),
        [VMEM] * (len(terms) + len(after)),
        (*terms, *after),
    )


def norm_kernel(place, gain_ref, hot_ref, *refs, parts, blocks):
    states, (sent_ref, own_ref, stat_ref) = refs[:-3], refs[-3:]
    chunk, width = states[0].shape
    gain = gain_ref[...].astype(jnp.float32)
    for m in range(parts):
        place_rows = slice(m * chunk, (m + 1) * chunk)
        rows = [states[k * parts + m][...].astype(jnp.float32) for k in range(blocks)]
        total = rows[0]
        for r in rows[1:]:
            total = total + r
        mean = jnp.sum(total, axis=-1, keepdims=True) / D
        rows = [r - mean for r in rows]
        total = rows[0] * rows[0]
        for r in rows[1:]:
            total = total + r * r
        variance = jnp.sum(total, axis=-1, keepdims=True) / D
        scale = lax.rsqrt(variance + 1e-05)
        own_ref[place_rows, :] = (rows[0] * scale * gain).astype(jnp.bfloat16)
        stat_ref[0, place_rows, :] = jnp.broadcast_to(mean, (chunk, HD))
        stat_ref[1, place_rows, :] = jnp.broadcast_to(scale, (chunk, HD))
    up_half(own_ref, hot_ref, place[2] ^ 1, sent_ref)


def up_half(rows_ref, hot_ref, half, out_ref):
    count = hot_ref.shape[0] // 2
    rows = rows_ref[...]
    for i in range(0, count, 2):
        at = half * count + i
        weight = jnp.concatenate([hot_ref[at], hot_ref[at + 1]], axis=1)
        out_ref[:, i * HD : (i + 2) * HD] = jnp.dot(
            rows, weight, preferred_element_type=jnp.float32
        ).astype(out_ref.dtype)


def norm(place, gain, hot, columns):
    blocks, parts = len(columns), len(columns[0])
    chunk, width = columns[0][0].shape
    rows = parts * chunk
    return call(
        functools.partial(norm_kernel, parts=parts, blocks=blocks),
        "norm_up_send",
        [
            like(rows, hot.shape[0] // 2 * HD),
            like(rows, width),
            jax.ShapeDtypeStruct((2, rows, HD), jnp.float32),
        ],
        [SMEM] + [VMEM] * (2 + blocks * parts),
        (place, gain, hot, *[a for column in columns for a in column]),
    )


def up_kernel(place, rows_ref, hot_ref, out_ref):
    up_half(rows_ref, hot_ref, place[2], out_ref)


def up_keep(place, rows, hot):
    return call(
        up_kernel,
        "up_keep",
        like(rows.shape[0], hot.shape[0] // 2 * HD),
        [SMEM, VMEM, VMEM],
        (place, rows, hot),
    )


def pieces_of(hidden, down_ref, block, width):
    depth = down_ref.shape[1]
    at = pl.ds(pl.multiple_of(block * width, width), width)
    weight = jnp.concatenate([down_ref[0, :, at], down_ref[1, :, at]], axis=0)
    return jnp.dot(hidden, weight, preferred_element_type=jnp.float32).astype(jnp.bfloat16)


def cold_kernel(place, counts, lists_ref, stat_ref, after, up_ref, down_ref, *refs, parts, steps):
    blocks = lists_ref.shape[0]
    gains, states = refs[:blocks], refs[blocks:-3]
    near_ref, out_ref, far_ref = refs[-3:]
    chunk, width = states[0].shape
    total = parts * chunk
    here = chunk // steps
    b = place[1]
    mean, scale = stat_ref[0][:, :1], stat_ref[1][:, :1]
    sums = jnp.zeros((total, 2 * HD), jnp.float32)
    for k in range(blocks):
        rows = jnp.concatenate(
            [states[k * parts + m][...] for m in range(parts)], axis=0
        ).astype(jnp.float32)
        gain = gains[k][...].astype(jnp.float32)
        normed = ((rows - mean) * scale * gain).astype(jnp.bfloat16)
        at = pl.ds(pl.multiple_of((b ^ k) * width, width), width)
        weight = jnp.concatenate([up_ref[0, at, :], up_ref[1, at, :]], axis=1)
        sums = sums + jnp.dot(normed, weight, preferred_element_type=jnp.float32)
    slots = lists_ref.shape[3]
    index = lax.broadcasted_iota(jnp.int32, (total, slots), 0)
    slot = lax.broadcasted_iota(jnp.int32, (total, slots), 1)
    owner = (index // chunk) ^ place[0]
    row = (index // here % steps) * (parts * here) + owner * here + index % here
    halves = []
    for c in range(2):
        hit = (row == lists_ref[b, 0, c : c + 1, :]) & (slot < counts[2 * b + c])
        used = jnp.max(jnp.where(hit, 1.0, 0.0), axis=-1, keepdims=True)
        halves.append((jnp.maximum(sums[:, c * HD : (c + 1) * HD], 0.0) * used))
    hidden = jnp.concatenate(halves, axis=1).astype(jnp.bfloat16)
    for i in range(blocks // 2):
        out_ref[i] = pieces_of(hidden, down_ref, b ^ (2 * i + 1), width)
    far_ref[...] = pieces_of(hidden, down_ref, b ^ 2, width)
    near_ref[...] = pieces_of(hidden, down_ref, b, width)


def cold_send(place, counts, lists, stat, after, cold_up, cold_down, gains, columns, steps):
    blocks, parts = len(columns), len(columns[0])
    chunk, width = columns[0][0].shape
    rows = parts * chunk
    flat = [a for column in columns for a in column]
    return call(
        functools.partial(cold_kernel, parts=parts, steps=steps),
        "cold_send",
        [
            like(rows, width),
            jax.ShapeDtypeStruct((blocks // 2, rows, width), jnp.bfloat16),
            like(rows, width),
        ],
        [SMEM, SMEM, VMEM, VMEM, AWAY, VMEM, VMEM] + [VMEM] * (blocks + len(flat)),
        (place, counts, lists, stat, after, cold_up, cold_down, *gains, *flat),
    )


def down_kernel(place, hidden_ref, partner_ref, hot_ref, *refs):
    count, depth = hot_ref.shape[0] // 2, hot_ref.shape[1]
    width = hot_ref.shape[2]
    wide = width // 3
    for i in range(3):
        column = slice(i * wide, (i + 1) * wide)
        made = refs[0][:, column].astype(jnp.float32)
        for ref in refs[1:-1]:
            made = made + ref[:, column].astype(jnp.float32)
        for half, rows_ref in enumerate((hidden_ref, partner_ref)):
            first = (place[2] ^ half) * count
            weight = hot_ref[pl.ds(first, count), :, column].reshape(count * depth, wide)
            made = made + jnp.dot(rows_ref[...], weight, preferred_element_type=jnp.float32)
        refs[-1][:, column] = made


def down(place, hidden, partner, hot, *before):
    return call(
        down_kernel,
        "down",
        like(hidden.shape[0], hot.shape[2], jnp.float32),
        [SMEM] + [VMEM] * (3 + len(before)),
        (place, hidden, partner, hot, *before),
    )


def chunks_kernel(base_ref, more_ref, *outs, first):
    chunk = outs[0].shape[0]
    for i, out in enumerate(outs):
        rows = slice(i * chunk, (i + 1) * chunk)
        from_base = slice((first + i) * chunk, (first + i + 1) * chunk)
        out[...] = (base_ref[from_base, :] + more_ref[rows, :].astype(jnp.float32)).astype(out.dtype)


def into_chunks(base, more, first, parts):
    width = base.shape[1]
    count = parts // 2
    chunk = more.shape[0] // count
    return call(
        functools.partial(chunks_kernel, first=first),
        "chunks_early" if first else "chunks_late",
        [like(chunk, width, jnp.bfloat16 if first + i else jnp.float32) for i in range(count)],
        [VMEM, VMEM],
        (base, more),
    )


def swap(x, axis, m, size=4):
    return lax.ppermute(x, axis, [(i, i ^ m) for i in range(size)])


def local_fast(
    queries,
    key_cache,
    value_cache,
    key_new,
    value_new,
    lengths,
    out_proj,
    residual,
    norm_gain,
    hot_up,
    hot_down,
    cold_up,
    cold_down,
    block_rows,
    block_counts,
):
    steps, here, _ = queries.shape
    all_rows, width = residual.shape[1:]
    parts = all_rows // here
    blocks = block_rows.shape[0]
    others = range(parts - 1, 0, -1)
    b = lax.axis_index("blocks")
    h = lax.axis_index("heads")
    place = jnp.stack([h, b, b % 2]).astype(jnp.int32)
    counts = block_counts.reshape(-1)

    attended = attention(queries, key_cache, value_cache, key_new, value_new, lengths)
    across = swap(attended, "blocks", 2)
    gathered = [join("hold", [attended]), swap(attended, "blocks", 1), across, swap(across, "blocks", 1)]
    gain = norm_gain[None]
    gains = [gain] + [swap(gain, "blocks", k) for k in range(1, blocks)]
    gathered, gains = lax.optimization_barrier((gathered, gains))
    pieces = project(place, gathered, out_proj)
    got = [swap(pieces[m], "heads", m) for m in others]
    (hot_up,) = load("load_up", pieces[1], hot_up)
    got, hot_up = lax.optimization_barrier((got, hot_up))
    mine = lax.dynamic_slice(residual, (0, h * here, 0), (steps, here, width))
    state = join("join", [mine.reshape(steps * here, width), pieces[0], *got])
    moved = {m: swap(state, "heads", m) for m in others}
    states = [state] + [moved[m] for m in range(1, parts)]
    across = [swap(s, "blocks", 2) for s in states]
    columns = [
        states,
        [swap(s, "blocks", 1) for s in states],
        across,
        [swap(s, "blocks", 1) for s in across],
    ]
    sent, own, stat = norm(place, gain, hot_up, columns)
    sent = swap(sent, "blocks", 1)
    kept = up_keep(place, own, hot_up)
    summed = join("join_hot", [kept, sent])
    arrived = swap(summed, "blocks", 2)

    near, cold_sent, far = cold_send(
        place, counts, block_rows, stat, summed, cold_up, cold_down, gains, columns, steps
    )
    cold_sent, arrived = lax.optimization_barrier((cold_sent, arrived))
    cold_got = swap(cold_sent, "blocks", 1)
    total = summed.astype(jnp.float32) + arrived.astype(jnp.float32)
    hidden = jnp.maximum(total, 0.0).astype(jnp.bfloat16)
    far = far.astype(jnp.float32) + cold_got[1].astype(jnp.float32)
    half = far.shape[0] // 2
    late, early = far[:half].astype(jnp.bfloat16), far[half:].astype(jnp.bfloat16)
    partner = swap(hidden, "blocks", 1)
    hidden, late, early = lax.optimization_barrier((hidden, late, early))
    early = swap(early, "blocks", 2)
    late = swap(late, "blocks", 2)
    base = down(place, hidden, partner, hot_down, near, cold_got[0])
    made = into_chunks(base, early, parts // 2, parts)
    arrived = [
        swap(made[i], "heads", parts // 2 + i) for i in reversed(range(parts // 2))
    ]
    made, late = lax.optimization_barrier((made, late))
    made = into_chunks(base, late, 0, parts)
    arrived += [swap(made[i], "heads", i) for i in range(1, parts // 2)]
    out = made[0]
    for piece in arrived:
        out = out + piece.astype(jnp.float32)
    ffn_out = out.astype(jnp.bfloat16).reshape(steps, here, width)

    stacked = jnp.stack(states).reshape(parts, steps, 1, here, width)
    ordered = [
        lax.dynamic_index_in_dim(stacked, c ^ h, axis=0, keepdims=False) for c in range(parts)
    ]
    attn_state = jnp.concatenate(ordered, axis=1).reshape(steps, all_rows, width)
    return (attn_state, ffn_out)


def solution(mesh):
    placed = (
        P(None, ("groups", "blocks"), "heads"),
        P(("groups", "blocks"), None, "heads"),
        P(("groups", "blocks"), None, "heads"),
        P(None, ("groups", "blocks"), "heads"),
        P(None, ("groups", "blocks"), "heads"),
        P(("groups", "blocks")),
        P("heads", "blocks"),
        P(None, "groups", "blocks"),
        P("blocks"),
        P("heads", "blocks", None),
        P("heads", None, "blocks"),
        P(("blocks", "heads"), None, None),
        P(("blocks", "heads"), None, None),
        P("groups", "heads", None, None),
        P("groups", "heads", None),
    )
    sizes = tuple(mesh.shape[a] for a in ("blocks", "heads"))
    return jax.shard_map(
        local_fast if sizes == (4, 4) else local,
        mesh=mesh,
        in_specs=placed,
        out_specs=(P(None, "groups", "blocks"), P(None, ("groups", "heads"), "blocks")),
        check_vma=False,
    )
```
